32 devices in a mesh: doc: 8 (over y, x, core), term: 4 (over z).
Axes of the slice: x: 2, y: 2, z: 4, core: 2. Of those that a mesh axis runs over, the one named last changes fastest.
Arguments:
- doc_tiles: bfloat16 [1024, 24, 2048], P('doc', None, 'term'), may hold values from -8 to 8
- tile_list: int32 [8, 24], replicated, may hold values from 0 to 127, as said below
Outputs:
- cosine: float32 [1024, 1024], P(('doc', 'term'))
The draws below stay inside these ranges and needn't reach their ends.
Inputs may be any that keep to these rules, and one draw needn't show every extreme that they name: `tile_list`: each row names 24 different term blocks.
All inputs are finite; a program needn't handle non-finite values.
Results may differ from the reference program's by a relative error of at most 0.0003.
Values may be sent and summed in bfloat16 or wider, within the bound.
A program may use at most 64 MiB of HBM per device.

```python
import jax
import jax.numpy as jnp
from jax import lax

ROWS = 128
TB = 2048
VOCAB = 262144
NNZ = 24
DOCS = 1024
N_TERM = 4


def term_choices(key):
    block_count = DOCS // ROWS
    block_kinds = VOCAB // TB
    favour_level = jax.random.randint(jax.random.fold_in(key, 11), (block_kinds,), 0, 4)
    jitter = jax.random.randint(jax.random.fold_in(key, 12), (block_count, block_kinds), 0, 2 ** 19)
    scores = (jitter + favour_level[None, :] * 2 ** 18) * block_kinds + jnp.arange(block_kinds, dtype=jnp.int32)[None, :]
    return lax.top_k(scores, NNZ)[1].astype(jnp.int32)


def draw_tile_list(key, part):
    return term_choices(key)


def draw_doc_tiles(key, part):
    block_count = DOCS // ROWS
    block_kinds = VOCAB // TB
    chosen = term_choices(key)
    profile = jax.random.normal(jax.random.fold_in(key, 21), (block_kinds, TB), jnp.float32)
    picked = profile[chosen]
    weights = jnp.exp(jax.random.uniform(jax.random.fold_in(key, 22), (block_count, ROWS, NNZ, 1), jnp.float32, -1.2, 0.7))
    roughness = 0.7 * jax.random.normal(jax.random.fold_in(key, 23), (block_count, ROWS, NNZ, TB), jnp.float32)
    values = weights * picked[:, None, :, :] + roughness
    return jnp.clip(values, -8.0, 8.0).reshape(DOCS, NNZ, TB).astype(jnp.bfloat16)


def setup_inputs(seed: int = 0) -> dict:
    streams_of = jax.random.split(jax.random.key(seed), 3)
    doc_tiles = draw_doc_tiles(jax.random.fold_in(streams_of[2], 71), 0)
    tile_list = draw_tile_list(jax.random.fold_in(streams_of[2], 71), 0)
    return {"doc_tiles": doc_tiles, "tile_list": tile_list}


epsilon = 1e-06

def reference(doc_tiles, tile_list):
    block_count = DOCS // ROWS
    term_width = TB // N_TERM
    blocks = doc_tiles.reshape(block_count, ROWS, NNZ, N_TERM, term_width)
    squares = lax.optimization_barrier(jnp.sum(jnp.square(doc_tiles.astype(jnp.float32)), axis=(1, 2)))
    row_norms = jnp.sqrt(squares + epsilon)

    def one_row(left_index):
        left_tiles = blocks[left_index].astype(jnp.float32)
        left_terms = tile_list[left_index]

        def one_pair(right_index):
            right_tiles = blocks[right_index].astype(jnp.float32)
            selector = (left_terms[:, None] == tile_list[right_index][None, :]).astype(jnp.float32)
            aligned = jnp.einsum('ab,sbtc->satc', selector, right_tiles)
            partial_sums = jnp.einsum('ratc,satc->trs', left_tiles, aligned)
            return lax.optimization_barrier(jnp.sum(partial_sums, axis=0))
        return lax.map(one_pair, jnp.arange(block_count, dtype=jnp.int32))
    gram_matrix = lax.map(one_row, jnp.arange(block_count, dtype=jnp.int32))
    gram_matrix = jnp.transpose(gram_matrix, (0, 2, 1, 3)).reshape(DOCS, DOCS)
    return gram_matrix / (row_norms[:, None] * row_norms[None, :])
```

```python
import functools

import jax
import jax.numpy as jnp
from jax import lax
from jax.experimental import pallas as pl
from jax.experimental.pallas import tpu as pltpu
from jax.sharding import PartitionSpec as P

epsilon = 1e-06
LANES = 128
MESH = pl.DeviceIdType.MESH


def body(
    D, T, G, C, N, R, L,
    table, chunks, out,
    tiles, part, got_xy, summed, got_z, sq_term, sq_doc,
    local_sem, send_a, recv_a, send_f, send_st, recv_st, send_sd, recv_sd,
    send_xy, recv_xy, send_z, recv_z,
):
    M = D // G
    SR = R // T
    CB = D // C
    CW = CB * R
    d = lax.axis_index("doc")
    t = lax.axis_index("term")
    g = lax.div(d, M)
    m = lax.rem(d, M)

    def doc_peer(o):
        return lax.rem(d + o, D)

    def term_peer(o):
        return lax.rem(t + o, T)

    def group_peer(o):
        return lax.rem(g + o, G) * M + m

    def member_peer(o):
        return g * M + lax.rem(m + o, M)

    def remote(src, dst, ssem, rsem, doc, term):
        return pltpu.make_async_remote_copy(
            src_ref=src, dst_ref=dst, send_sem=ssem, recv_sem=rsem,
            device_id=(doc, term), device_id_type=MESH,
        )

    def block_of(b):
        return tiles.at[pl.ds(b * N, N)]

    barrier = pltpu.get_barrier_semaphore()
    for o in range(1, D):
        pl.semaphore_signal(barrier, inc=1, device_id=(doc_peer(o), t), device_id_type=MESH)
    for o in range(1, T):
        pl.semaphore_signal(barrier, inc=1, device_id=(d, term_peer(o)), device_id_type=MESH)
    if D + T > 2:
        pl.semaphore_wait(barrier, D + T - 2)

    pending = []

    for o in range(1, G):
        to = lax.rem(g + o, G)
        copy = remote(chunks.at[pl.ds(to * N, N)], block_of(d), send_a.at[o - 1], recv_a.at[d], to * M + m, t)
        copy.start()
        pending.append(copy)
    mine = pltpu.make_async_copy(chunks.at[pl.ds(g * N, N)], block_of(d), local_sem)
    mine.start()
    for o in range(1, M):
        copy = remote(
            chunks.at[pl.ds(g * N, N)], block_of(d), send_f.at[0, o - 1], recv_a.at[d], member_peer(o), t
        )
        copy.start()
        pending.append(copy)

    tiles[D * N] = jnp.zeros((R, L), tiles.dtype)

    def add_square(i, total):
        value = chunks[i].astype(jnp.float32)
        return total + value * value

    square = lax.fori_loop(0, G * N, add_square, jnp.zeros((R, L), jnp.float32))
    column = jnp.sum(square, axis=1, keepdims=True)
    eye = lax.broadcasted_iota(jnp.int32, (R, R), 0) == lax.broadcasted_iota(jnp.int32, (R, R), 1)
    row = jnp.sum(jnp.where(eye, column, 0.0), axis=0, keepdims=True)
    sq_term[t] = jnp.broadcast_to(row, (8, R))
    for o in range(1, T):
        copy = remote(sq_term.at[t], sq_term.at[t], send_st.at[o - 1], recv_st.at[t], d, term_peer(o))
        copy.start()
        pending.append(copy)
    for o in range(1, T):
        p = term_peer(o)
        remote(sq_term.at[p], sq_term.at[p], send_st.at[o - 1], recv_st.at[p], d, p).wait_recv()
    total = sq_term[0]
    for q in range(1, T):
        total = total + sq_term[q]
    sq_doc[d] = total
    for o in range(1, D):
        copy = remote(sq_doc.at[d], sq_doc.at[d], send_sd.at[o - 1], recv_sd.at[d], doc_peer(o), t)
        copy.start()
        pending.append(copy)

    for o in range(1, G):
        b = group_peer(G - o)
        remote(block_of(b), block_of(b), send_a.at[o - 1], recv_a.at[b], b, t).wait_recv()
        for i in range(1, M):
            copy = remote(block_of(b), block_of(b), send_f.at[o, i - 1], recv_a.at[b], member_peer(i), t)
            copy.start()
            pending.append(copy)
    mine.wait()
    for o in range(G):
        for i in range(1, M):
            b = lax.rem(g + G - o, G) * M + lax.rem(m + i, M)
            remote(block_of(b), block_of(b), send_f.at[o, i - 1], recv_a.at[b], member_peer(i), t).wait_recv()

    for ch in range(C):
        def one_block(k, carry, ch=ch):
            c = ch * CB + k
            right = jnp.concatenate([tiles[c * N + e] for e in range(N)], axis=1)
            for j in range(G):
                left = jnp.concatenate(
                    [tiles[table[(j * D + c) * N + e]] for e in range(N)], axis=1
                )
                part[ch, j, :, pl.ds(pl.multiple_of(k * R, R), R)] = lax.dot_general(
                    left, right, (((1,), (1,)), ((), ())), preferred_element_type=jnp.float32
                )
            return carry

        lax.fori_loop(0, CB, one_block, 0)
        for o in range(1, G):
            copy = remote(
                part.at[ch, o], got_xy.at[ch, o - 1], send_xy.at[ch, o - 1], recv_xy.at[ch, o - 1],
                group_peer(o), t,
            )
            copy.start()
            pending.append(copy)

    for ch in range(C):
        for o in range(1, G):
            remote(
                part.at[ch, o], got_xy.at[ch, o - 1], send_xy.at[ch, o - 1], recv_xy.at[ch, o - 1],
                group_peer(o), t,
            ).wait_recv()
        for q in range(T):
            rows = pl.ds(q * SR, SR)
            total = part[ch, 0, rows, :]
            for o in range(1, G):
                total = total + got_xy[ch, o - 1, rows, :]
            summed[ch, q] = total
        for o in range(1, T):
            p = term_peer(o)
            copy = remote(
                summed.at[ch, p], got_z.at[ch, o - 1], send_z.at[ch, o - 1], recv_z.at[ch, o - 1], d, p
            )
            copy.start()
            pending.append(copy)

    for o in range(1, D):
        p = doc_peer(o)
        remote(sq_doc.at[p], sq_doc.at[p], send_sd.at[o - 1], recv_sd.at[p], p, t).wait_recv()
    own = sq_doc[d][0:1]
    pick = lax.broadcasted_iota(jnp.int32, (SR, R), 1) == (
        lax.broadcasted_iota(jnp.int32, (SR, R), 0) + t * SR
    )
    own_column = jnp.sum(jnp.where(pick, own, 0.0), axis=1, keepdims=True)
    row_norm = jnp.sqrt(own_column + epsilon)
    for ch in range(C):
        for o in range(1, T):
            remote(
                summed.at[ch, t], got_z.at[ch, o - 1], send_z.at[ch, o - 1], recv_z.at[ch, o - 1],
                d, term_peer(o),
            ).wait_recv()
        total = summed[ch, t]
        for o in range(1, T):
            total = total + got_z[ch, o - 1]
        squares = jnp.concatenate([sq_doc[ch * CB + k, 0:1, :] for k in range(CB)], axis=1)
        out[:, ch * CW : (ch + 1) * CW] = total / (row_norm * jnp.sqrt(squares + epsilon))

    for copy in pending:
        copy.wait_send()


def shards(doc_tiles, tile_list):
    D = lax.axis_size("doc")
    T = lax.axis_size("term")
    R, N, W = doc_tiles.shape
    G = W // LANES
    while D % G or W % G:
        G -= 1
    L = W // G
    M = D // G
    C = 4 if D % 4 == 0 else 1
    SR = R // T
    CW = D // C * R
    d = lax.axis_index("doc")
    rows = (d // M + jnp.arange(G, dtype=jnp.int32)) % G * M + d % M
    matches = tile_list[rows][:, None, None, :] == tile_list[None, :, :, None]
    places = rows[:, None] * N + jnp.arange(N, dtype=jnp.int32)[None, :]
    table = jnp.min(jnp.where(matches, places[:, None, None, :], D * N), axis=3).reshape(-1)
    chunks = jnp.transpose(doc_tiles.reshape(R, N, G, L), (2, 1, 0, 3)).reshape(G * N, R, L)
    many = lambda *shape: pltpu.SemaphoreType.DMA(tuple(max(n, 1) for n in shape))
    buffer = lambda *shape: pltpu.VMEM(tuple(max(n, 1) for n in shape), jnp.float32)
    return pl.pallas_call(
        functools.partial(body, D, T, G, C, N, R, L),
        out_shape=jax.ShapeDtypeStruct((SR, D * R), jnp.float32),
        in_specs=[
            pl.BlockSpec(memory_space=pltpu.SMEM),
            pl.BlockSpec(memory_space=pltpu.VMEM),
        ],
        out_specs=pl.BlockSpec(memory_space=pltpu.VMEM),
        scratch_shapes=[
            pltpu.VMEM((D * N + 1, R, L), doc_tiles.dtype),
            buffer(C, G, R, CW),
            buffer(C, G - 1, R, CW),
            buffer(C, T, SR, CW),
            buffer(C, T - 1, SR, CW),
            buffer(T, 8, R),
            buffer(D, 8, R),
            pltpu.SemaphoreType.DMA,
            many(G - 1), many(D), many(G, M - 1),
            many(T - 1), many(T), many(D - 1), many(D),
            many(C, G - 1), many(C, G - 1), many(C, T - 1), many(C, T - 1),
        ],
        compiler_params=pltpu.CompilerParams(
            collective_id=0, has_side_effects=True, vmem_limit_bytes=56 * 1024 * 1024
        ),
        cost_estimate=pl.CostEstimate(
            flops=2 * G * R * D * R * N * L,
            bytes_accessed=R * N * W * 2 + SR * D * R * 4,
            transcendentals=0,
        ),
    )(table, chunks)


def solution(mesh):
    placed = (P("doc", None, "term"), P())
    return jax.shard_map(
        shards, mesh=mesh, in_specs=placed, out_specs=P(("doc", "term"), None), check_vma=False
    )
```

```python
import functools

import jax
import jax.numpy as jnp
from jax import lax
from jax.experimental import pallas as pl
from jax.experimental.pallas import tpu as pltpu
from jax.sharding import PartitionSpec as P

epsilon = 1e-06
LANES = 128
MESH = pl.DeviceIdType.MESH


def flip(g, o):
    bit = 1
    while bit <= o:
        if o & bit:
            g = g + bit - 2 * bit * lax.rem(lax.div(g, bit), 2)
        bit *= 2
    return g


class Plan:
    def __init__(self, D, T, R, N, W):
        G = 1
        while D % (2 * G) == 0 and W % (2 * G * LANES) == 0:
            G *= 2
        self.D, self.T, self.R, self.N, self.W, self.G = D, T, R, N, W, G
        self.M = D // G
        self.L = W // G
        self.SR = R // T
        self.mirrored = G > 1 and self.M % 2 == 0
        self.H = self.M // 2 if self.mirrored else self.M

    def count(self, o):
        return self.M if o == 0 else self.H

    def stage(self, o):
        return 0 if o == 0 else 1 if o & (o - 1) == 0 else 2


def body(plan, table, chunks, out, *scratch):
    D, T, G, M, H = plan.D, plan.T, plan.G, plan.M, plan.H
    R, N, L, SR = plan.R, plan.N, plan.L, plan.SR
    scratch = list(scratch)
    take = lambda n: [scratch.pop(0) for _ in range(n)]
    tiles = take(G)
    part = {(a, b): take(1)[0] for a in range(G) for b in range(G)}
    got = {(a, b): take(1)[0] for a in range(1, G) for b in range(G)}
    whole = {b: take(1)[0] for b in range(G)}
    got_z = {b: take(1)[0] for b in range(G)}
    if plan.mirrored:
        turned = {b: take(1)[0] for b in range(1, G)}
        mirror = {b: take(1)[0] for b in range(1, G)}
        got_mz = {b: take(1)[0] for b in range(1, G)}
    own, sq_term, sq_doc = take(3)
    (
        local_sem, own_sem, send_a, recv_a, send_f, send_st, recv_st, send_sd, recv_sd,
        send_p, recv_p, send_m, recv_m, send_z, recv_z, send_mz, recv_mz,
    ) = scratch

    d = lax.axis_index("doc")
    t = lax.axis_index("term")
    g = lax.div(d, M)
    m = lax.rem(d, M)
    groups = [flip(g, o) for o in range(G)]

    def doc_peer(o):
        return lax.rem(d + o, D)

    def term_peer(o):
        return lax.rem(t + o, T)

    def sibling(i):
        return lax.rem(m + i, M)

    def remote(src, dst, ssem, rsem, doc, term):
        return pltpu.make_async_remote_copy(
            src_ref=src, dst_ref=dst, send_sem=ssem, recv_sem=rsem,
            device_id=(doc, term), device_id_type=MESH,
        )

    def column_member(row_group, column_group, i):
        if not plan.mirrored:
            return i
        return 2 * i + lax.rem(m + jnp.where(row_group < column_group, 1, 0), 2)

    def slot(o, member):
        return tiles[o].at[pl.ds(member * N, N)]

    def cut(group):
        if G == 1:
            return chunks
        return chunks.at[:, :, pl.ds(pl.multiple_of(group * L, L), L)]

    barrier = pltpu.get_barrier_semaphore()
    for o in range(1, D):
        pl.semaphore_signal(barrier, inc=1, device_id=(doc_peer(o), t), device_id_type=MESH)
    for o in range(1, T):
        pl.semaphore_signal(barrier, inc=1, device_id=(d, term_peer(o)), device_id_type=MESH)
    if D + T > 2:
        pl.semaphore_wait(barrier, D + T - 2)

    pending = []

    def begin(copy):
        copy.start()
        pending.append(copy)
        return copy

    def send_range(o):
        return begin(
            remote(
                cut(groups[o]), slot(o, m), send_a.at[o], recv_a.at[o, m], groups[o] * M + m, t
            )
        )

    def hand_on(o, source):
        for i in range(1, M):
            begin(
                remote(
                    source, slot(o, m), send_f.at[o, i], recv_a.at[o, m], g * M + sibling(i), t
                )
            )

    def take_over(o):
        for i in range(1, M):
            other = sibling(i)
            remote(
                slot(o, other), slot(o, other), send_f.at[o, i], recv_a.at[o, other], g * M + other, t
            ).wait_recv()

    def arrived(o):
        remote(
            slot(o, m), slot(o, m), send_a.at[o], recv_a.at[o, m], groups[o] * M + m, t
        ).wait_recv()
        hand_on(o, slot(o, m))

    first = [o for o in range(1, G) if plan.stage(o) == 1]
    second = [o for o in range(1, G) if plan.stage(o) == 2]
    first_sends = [send_range(o) for o in first]
    mine = pltpu.make_async_copy(cut(g), slot(0, m), local_sem)
    mine.start()
    hand_on(0, cut(g))
    all_own = pltpu.make_async_copy(chunks, own, own_sem)
    all_own.start()

    for o in range(G):
        tiles[o][M * N] = jnp.zeros((R, L), own.dtype)
    all_own.wait()

    def add_square(a, total):
        for q in range(G):
            value = own[a, :, q * L : (q + 1) * L].astype(jnp.float32)
            total = total + value * value
        return total

    square = lax.fori_loop(0, N, add_square, jnp.zeros((R, L), jnp.float32))
    column = jnp.sum(square, axis=1, keepdims=True)
    eye = lax.broadcasted_iota(jnp.int32, (R, R), 0) == lax.broadcasted_iota(jnp.int32, (R, R), 1)
    row = jnp.sum(jnp.where(eye, column, 0.0), axis=0, keepdims=True)
    sq_term[t] = jnp.broadcast_to(row, (8, R))
    for o in range(1, T):
        begin(remote(sq_term.at[t], sq_term.at[t], send_st.at[o], recv_st.at[t], d, term_peer(o)))
    for o in range(1, T):
        p = term_peer(o)
        remote(sq_term.at[p], sq_term.at[p], send_st.at[o], recv_st.at[p], d, p).wait_recv()
    total = sq_term[0]
    for q in range(1, T):
        total = total + sq_term[q]
    sq_doc[d] = total
    for o in range(1, D):
        begin(remote(sq_doc.at[d], sq_doc.at[d], send_sd.at[o], recv_sd.at[d], doc_peer(o), t))

    def pair(a, b):
        row_block = groups[a] * M + m

        def one(i, carry):
            member = i if a == b else column_member(groups[a], groups[b], i)
            line = row_block * D + groups[b] * M + member
            left = jnp.concatenate([tiles[a][table[line, e]] for e in range(N)], axis=1)
            right = jnp.concatenate([tiles[b][member * N + e] for e in range(N)], axis=1)
            part[a, b][i] = lax.dot_general(
                left, right, (((1,), (1,)), ((), ())), preferred_element_type=jnp.float32
            )
            return carry

        number = plan.count(a ^ b)
        if number == 1:
            one(0, 0)
        else:
            lax.fori_loop(0, number, one, 0)
        if a:
            begin(
                remote(
                    part[a, b], got[a, b], send_p.at[a, b], recv_p.at[a, b], groups[a] * M + m, t
                )
            )

    wanted = list(range(1, G)) + [0]

    def pairs(stage):
        todo = [
            (a, b)
            for a in range(G)
            for b in range(G)
            if max(plan.stage(a), plan.stage(b)) == stage
        ]
        for a, b in sorted(todo, key=lambda ab: (wanted.index(ab[0] ^ ab[1]), -ab[0])):
            pair(a, b)

    mine.wait()
    take_over(0)
    pairs(0)
    for o in first:
        arrived(o)
    for copy in first_sends:
        copy.wait_send()
        pending.remove(copy)
    for o in second:
        send_range(o)
    for o in first:
        take_over(o)
    if first:
        pairs(1)
    for o in second:
        arrived(o)
    for o in second:
        take_over(o)
    if second:
        pairs(2)

    def over_term(source, landing, ssem, rsem):
        for o in range(1, T):
            p = term_peer(o)
            begin(
                remote(
                    source.at[:, pl.ds(p * SR, SR), :], landing.at[o - 1], ssem.at[o], rsem.at[o], d, p
                )
            )

    for b in wanted:
        for a in range(1, G):
            remote(
                part[a, a ^ b], got[a, a ^ b], send_p.at[a, a ^ b], recv_p.at[a, a ^ b],
                groups[a] * M + m, t,
            ).wait_recv()
        for i in range(plan.count(b)):
            total = part[0, b][i]
            for a in range(1, G):
                total = total + got[a, a ^ b][i]
            whole[b][i] = total
            if plan.mirrored and b:
                turned[b][i] = total.T
                begin(
                    remote(
                        turned[b].at[i], mirror[b].at[lax.div(m, 2)], send_m.at[b, i],
                        recv_m.at[b, lax.div(m, 2)],
                        groups[b] * M + column_member(g, groups[b], i), t,
                    )
                )
        over_term(whole[b], got_z[b], send_z.at[b], recv_z.at[b])

    def mirror_member(b, i):
        return 2 * i + lax.rem(m + jnp.where(groups[b] < g, 1, 0), 2)

    if plan.mirrored:
        for b in range(1, G):
            for i in range(H):
                remote(
                    turned[b].at[i], mirror[b].at[i], send_m.at[b, i], recv_m.at[b, i],
                    groups[b] * M + mirror_member(b, i), t,
                ).wait_recv()
            over_term(mirror[b], got_mz[b], send_mz.at[b], recv_mz.at[b])

    for o in range(1, D):
        p = doc_peer(o)
        remote(sq_doc.at[p], sq_doc.at[p], send_sd.at[o], recv_sd.at[p], p, t).wait_recv()
    pick = lax.broadcasted_iota(jnp.int32, (SR, R), 1) == (
        lax.broadcasted_iota(jnp.int32, (SR, R), 0) + t * SR
    )
    own_column = jnp.sum(jnp.where(pick, sq_doc[d][0:1], 0.0), axis=1, keepdims=True)
    row_norm = jnp.sqrt(own_column + epsilon)

    def finish(source, landing, ssem, rsem, number, block):
        for o in range(1, T):
            remote(
                source.at[:, pl.ds(t * SR, SR), :], landing.at[o - 1], ssem.at[o], rsem.at[o],
                d, term_peer(o),
            ).wait_recv()
        for i in range(number):
            total = source[i, pl.ds(pl.multiple_of(t * SR, SR), SR), :]
            for o in range(1, T):
                total = total + landing[o - 1, i]
            c = block(i)
            norms = row_norm * jnp.sqrt(sq_doc[c][0:1] + epsilon)
            out[:, pl.ds(pl.multiple_of(c * R, R), R)] = total / norms

    for b in wanted:
        finish(
            whole[b], got_z[b], send_z.at[b], recv_z.at[b], plan.count(b),
            lambda i, b=b: groups[b] * M + (column_member(g, groups[b], i) if b else i),
        )
    if plan.mirrored:
        for b in range(1, G):
            finish(
                mirror[b], got_mz[b], send_mz.at[b], recv_mz.at[b], H,
                lambda i, b=b: groups[b] * M + mirror_member(b, i),
            )

    for copy in pending:
        copy.wait_send()


def shards(doc_tiles, tile_list):
    D = lax.axis_size("doc")
    T = lax.axis_size("term")
    R, N, W = doc_tiles.shape
    plan = Plan(D, T, R, N, W)
    G, M, H, L, SR = plan.G, plan.M, plan.H, plan.L, plan.SR
    matches = tile_list[:, None, None, :] == tile_list[None, :, :, None]
    places = (jnp.arange(D, dtype=jnp.int32) % M)[:, None] * N + jnp.arange(N, dtype=jnp.int32)
    table = jnp.min(jnp.where(matches, places[:, None, None, :], M * N), axis=3).reshape(D * D, N)
    chunks = jnp.transpose(doc_tiles, (1, 0, 2))
    many = lambda *shape: pltpu.SemaphoreType.DMA(shape)
    buffer = lambda *shape: pltpu.VMEM(tuple(max(n, 1) for n in shape), jnp.float32)
    scratch = [pltpu.VMEM((M * N + 1, R, L), doc_tiles.dtype) for _ in range(G)]
    scratch += [buffer(plan.count(a ^ b), R, R) for a in range(G) for b in range(G)]
    scratch += [buffer(plan.count(a ^ b), R, R) for a in range(1, G) for b in range(G)]
    scratch += [buffer(plan.count(b), R, R) for b in range(G)]
    scratch += [buffer(T - 1, plan.count(b), SR, R) for b in range(G)]
    if plan.mirrored:
        scratch += [buffer(H, R, R) for _ in range(1, G)]
        scratch += [buffer(H, R, R) for _ in range(1, G)]
        scratch += [buffer(T - 1, H, SR, R) for _ in range(1, G)]
    scratch += [pltpu.VMEM((N, R, W), doc_tiles.dtype), buffer(T, 8, R), buffer(D, 8, R)]
    scratch += [
        pltpu.SemaphoreType.DMA, pltpu.SemaphoreType.DMA,
        many(G), many(G, M), many(G, M),
        many(T), many(T), many(D), many(D),
        many(G, G), many(G, G), many(G, M), many(G, M),
        many(G, T), many(G, T), many(G, T), many(G, T),
    ]
    return pl.pallas_call(
        functools.partial(body, plan),
        out_shape=jax.ShapeDtypeStruct((SR, D * R), jnp.float32),
        in_specs=[
            pl.BlockSpec(memory_space=pltpu.SMEM),
            pl.BlockSpec(memory_space=pl.ANY),
        ],
        out_specs=pl.BlockSpec(memory_space=pltpu.VMEM),
        scratch_shapes=scratch,
        compiler_params=pltpu.CompilerParams(
            collective_id=0, has_side_effects=True, vmem_limit_bytes=56 * 1024 * 1024
        ),
        cost_estimate=pl.CostEstimate(
            flops=2 * G * R * D * R * N * L,
            bytes_accessed=R * N * W * 2 + SR * D * R * 4,
            transcendentals=0,
        ),
    )(table, chunks)


def solution(mesh):
    placed = (P("doc", None, "term"), P())
    return jax.shard_map(
        shards, mesh=mesh, in_specs=placed, out_specs=P(("doc", "term"), None), check_vma=False
    )
```

```python
import functools

import jax
import jax.numpy as jnp
from jax import lax
from jax.experimental import pallas as pl
from jax.experimental.pallas import tpu as pltpu
from jax.sharding import PartitionSpec as P

epsilon = 1e-06
LANES = 128
MESH = pl.DeviceIdType.MESH


def flip(g, o):
    bit = 1
    while bit <= o:
        if o & bit:
            g = g + bit - 2 * bit * lax.rem(lax.div(g, bit), 2)
        bit *= 2
    return g


class Plan:
    def __init__(self, D, T, R, N, W):
        G = 1
        while D % (2 * G) == 0 and W % (2 * G * LANES) == 0:
            G *= 2
        self.D, self.T, self.R, self.N, self.W, self.G = D, T, R, N, W, G
        self.M = D // G
        self.L = W // G
        self.SR = R // T
        self.mirrored = G > 1 and self.M % 2 == 0
        self.H = self.M // 2 if self.mirrored else self.M
        self.parts = 2 if N % 2 == 0 else 1
        self.step = N // self.parts
        self.rows = 16 if R % 16 == 0 else R

    def count(self, o):
        return self.M if o == 0 else self.H

    def stage(self, o):
        return 0 if o == 0 else 1 if o & (o - 1) == 0 else 2


def body(plan, names, docs, out, *scratch):
    D, T, G, M, H = plan.D, plan.T, plan.G, plan.M, plan.H
    R, N, L, SR = plan.R, plan.N, plan.L, plan.SR
    scratch = list(scratch)
    take = lambda n: [scratch.pop(0) for _ in range(n)]
    tiles = take(G)
    part = {(a, b): take(1)[0] for a in range(G) for b in range(G)}
    got = {(a, b): take(1)[0] for a in range(1, G) for b in range(G)}
    whole = {b: take(1)[0] for b in range(G)}
    got_z = {b: take(1)[0] for b in range(G)}
    if plan.mirrored:
        turned = {b: take(1)[0] for b in range(1, G)}
        mirror = {b: take(1)[0] for b in range(1, G)}
        got_mz = {b: take(1)[0] for b in range(1, G)}
    raw = take(G)
    ranges = [None] + take(G - 1)
    sq_term, sq_doc, table_rows, table = take(4)
    (
        raw_sem, table_sem, send_a, recv_a, send_f, send_st, recv_st, send_sd, recv_sd,
        send_p, recv_p, send_m, recv_m, send_z, recv_z, send_mz, recv_mz,
    ) = scratch

    d = lax.axis_index("doc")
    t = lax.axis_index("term")
    g = lax.div(d, M)
    m = lax.rem(d, M)
    groups = [flip(g, o) for o in range(G)]

    def doc_peer(o):
        return lax.rem(d + o, D)

    def term_peer(o):
        return lax.rem(t + o, T)

    def sibling(i):
        return lax.rem(m + i, M)

    def remote(src, dst, ssem, rsem, doc, term):
        return pltpu.make_async_remote_copy(
            src_ref=src, dst_ref=dst, send_sem=ssem, recv_sem=rsem,
            device_id=(doc, term), device_id_type=MESH,
        )

    def column_member(row_group, column_group, i):
        if not plan.mirrored:
            return i
        return 2 * i + lax.rem(m + jnp.where(row_group < column_group, 1, 0), 2)

    parts, step = plan.parts, plan.step

    def slot(o, member, h):
        return tiles[o].at[pl.ds(member * (N + 1) + h * step, step)]

    def cut(group):
        if G == 1:
            return docs
        return docs.at[:, :, pl.ds(pl.multiple_of(group * L, L), L)]

    first = [o for o in range(1, G) if plan.stage(o) == 1]
    second = [o for o in range(1, G) if plan.stage(o) == 2]
    loads = {}
    for o in first + [0] + second:
        loads[o] = pltpu.make_async_copy(cut(groups[o]), raw[o], raw_sem.at[o])
        loads[o].start()

    barrier = pltpu.get_barrier_semaphore()
    for o in range(1, D):
        pl.semaphore_signal(barrier, inc=1, device_id=(doc_peer(o), t), device_id_type=MESH)
    for o in range(1, T):
        pl.semaphore_signal(barrier, inc=1, device_id=(d, term_peer(o)), device_id_type=MESH)
    if D + T > 2:
        pl.semaphore_wait(barrier, D + T - 2)

    pending = []

    def begin(copy):
        copy.start()
        pending.append(copy)
        return copy

    def send_range(o, h):
        return begin(
            remote(
                ranges[o].at[pl.ds(h * step, step)], slot(o, m, h), send_a.at[o, h],
                recv_a.at[o, m, h], groups[o] * M + m, t,
            )
        )

    def hand_on(o, h):
        for i in range(1, M):
            begin(
                remote(
                    slot(o, m, h), slot(o, m, h), send_f.at[o, i, h], recv_a.at[o, m, h],
                    g * M + sibling(i), t,
                )
            )

    def take_over(o):
        for h in range(parts):
            for i in range(1, M):
                other = sibling(i)
                remote(
                    slot(o, other, h), slot(o, other, h), send_f.at[o, i, h], recv_a.at[o, other, h],
                    g * M + other, t,
                ).wait_recv()

    def arrived(o, h):
        remote(
            slot(o, m, h), slot(o, m, h), send_a.at[o, h], recv_a.at[o, m, h], groups[o] * M + m, t
        ).wait_recv()
        hand_on(o, h)

    def slots_first(o):
        loads[o].wait()

        def some_rows(k, carry):
            rows = pl.ds(pl.multiple_of(k * plan.rows, plan.rows), plan.rows)
            value = jnp.transpose(raw[o][rows], (1, 0, 2))
            if o:
                ranges[o][:, rows, :] = value
            else:
                tiles[0][pl.ds(m * (N + 1), N), rows, :] = value
            return carry

        lax.fori_loop(0, R // plan.rows, some_rows, 0)

    first_sends = []
    for o in first:
        slots_first(o)
        for h in range(parts):
            first_sends.append(send_range(o, h))
    slots_first(0)
    for h in range(parts):
        hand_on(0, h)
    for o in second:
        slots_first(o)
        for h in range(parts - 1):
            send_range(o, h)

    for o in range(G):
        tiles[o][m * (N + 1) + N] = jnp.zeros((R, L), docs.dtype)
    same = lax.broadcasted_iota(jnp.int32, (N, N), 0) == lax.broadcasted_iota(jnp.int32, (N, N), 1)
    place = lax.broadcasted_iota(jnp.int32, (N, N), 0)
    for a in range(G):
        line = names[pl.ds(groups[a] * M + m, 1), :]
        upright = jnp.sum(jnp.where(same, line, 0), axis=1, keepdims=True)
        for c in range(D):
            found = jnp.where(upright == names[c : c + 1, :], place, N)
            table_rows[a * D + c : a * D + c + 1, 0:N] = jnp.min(found, axis=0, keepdims=True)
    to_scalars = pltpu.make_async_copy(table_rows, table, table_sem)
    to_scalars.start()

    def add_square(a, total):
        for q in range(G):
            held = ranges[q][a] if q else tiles[0][m * (N + 1) + a]
            value = held.astype(jnp.float32)
            total = total + value * value
        return total

    square = lax.fori_loop(0, N, add_square, jnp.zeros((R, L), jnp.float32))
    column = jnp.sum(square, axis=1, keepdims=True)
    eye = lax.broadcasted_iota(jnp.int32, (R, R), 0) == lax.broadcasted_iota(jnp.int32, (R, R), 1)
    row = jnp.sum(jnp.where(eye, column, 0.0), axis=0, keepdims=True)
    sq_term[t] = jnp.broadcast_to(row, (8, R))
    for o in range(1, T):
        begin(remote(sq_term.at[t], sq_term.at[t], send_st.at[o], recv_st.at[t], d, term_peer(o)))
    for o in range(1, T):
        p = term_peer(o)
        remote(sq_term.at[p], sq_term.at[p], send_st.at[o], recv_st.at[p], d, p).wait_recv()
    total = sq_term[0]
    for q in range(1, T):
        total = total + sq_term[q]
    sq_doc[d] = total
    for o in range(1, D):
        begin(remote(sq_doc.at[d], sq_doc.at[d], send_sd.at[o], recv_sd.at[d], doc_peer(o), t))

    def pair(a, b):
        def one(i, carry):
            member = i if a == b else column_member(groups[a], groups[b], i)
            line = a * D + groups[b] * M + member
            left = jnp.concatenate(
                [tiles[a][m * (N + 1) + table[line, e]] for e in range(N)], axis=1
            )
            right = jnp.concatenate([tiles[b][member * (N + 1) + e] for e in range(N)], axis=1)
            part[a, b][i] = lax.dot_general(
                left, right, (((1,), (1,)), ((), ())), preferred_element_type=jnp.float32
            )
            return carry

        number = plan.count(a ^ b)
        if number == 1:
            one(0, 0)
        else:
            lax.fori_loop(0, number, one, 0)
        if a:
            begin(
                remote(
                    part[a, b], got[a, b], send_p.at[a, b], recv_p.at[a, b], groups[a] * M + m, t
                )
            )

    wanted = list(range(1, G)) + [0]

    def pairs(stage):
        todo = [
            (a, b)
            for a in range(G)
            for b in range(G)
            if max(plan.stage(a), plan.stage(b)) == stage
        ]
        for a, b in sorted(todo, key=lambda ab: (wanted.index(ab[0] ^ ab[1]), -ab[0])):
            pair(a, b)

    to_scalars.wait()
    take_over(0)
    pairs(0)
    for h in range(parts):
        for o in first:
            arrived(o, h)
    for copy in first_sends:
        copy.wait_send()
        pending.remove(copy)
    for o in second:
        send_range(o, parts - 1)
    for o in first:
        take_over(o)
    if first:
        pairs(1)
    for h in range(parts):
        for o in second:
            arrived(o, h)
    for o in second:
        take_over(o)
    if second:
        pairs(2)

    def over_term(source, landing, ssem, rsem):
        for o in range(1, T):
            p = term_peer(o)
            begin(
                remote(
                    source.at[:, pl.ds(p * SR, SR), :], landing.at[o - 1], ssem.at[o], rsem.at[o], d, p
                )
            )

    for b in wanted:
        for a in range(1, G):
            remote(
                part[a, a ^ b], got[a, a ^ b], send_p.at[a, a ^ b], recv_p.at[a, a ^ b],
                groups[a] * M + m, t,
            ).wait_recv()
        for i in range(plan.count(b)):
            total = part[0, b][i]
            for a in range(1, G):
                total = total + got[a, a ^ b][i]
            whole[b][i] = total
            if plan.mirrored and b:
                turned[b][i] = total.T
                begin(
                    remote(
                        turned[b].at[i], mirror[b].at[lax.div(m, 2)], send_m.at[b, i],
                        recv_m.at[b, lax.div(m, 2)],
                        groups[b] * M + column_member(g, groups[b], i), t,
                    )
                )
        over_term(whole[b], got_z[b], send_z.at[b], recv_z.at[b])

    def mirror_member(b, i):
        return 2 * i + lax.rem(m + jnp.where(groups[b] < g, 1, 0), 2)

    if plan.mirrored:
        for b in range(1, G):
            for i in range(H):
                remote(
                    turned[b].at[i], mirror[b].at[i], send_m.at[b, i], recv_m.at[b, i],
                    groups[b] * M + mirror_member(b, i), t,
                ).wait_recv()
            over_term(mirror[b], got_mz[b], send_mz.at[b], recv_mz.at[b])

    for o in range(1, D):
        p = doc_peer(o)
        remote(sq_doc.at[p], sq_doc.at[p], send_sd.at[o], recv_sd.at[p], p, t).wait_recv()
    pick = lax.broadcasted_iota(jnp.int32, (SR, R), 1) == (
        lax.broadcasted_iota(jnp.int32, (SR, R), 0) + t * SR
    )
    own_column = jnp.sum(jnp.where(pick, sq_doc[d][0:1], 0.0), axis=1, keepdims=True)
    row_norm = jnp.sqrt(own_column + epsilon)

    def finish(source, landing, ssem, rsem, number, block):
        for o in range(1, T):
            remote(
                source.at[:, pl.ds(t * SR, SR), :], landing.at[o - 1], ssem.at[o], rsem.at[o],
                d, term_peer(o),
            ).wait_recv()
        for i in range(number):
            total = source[i, pl.ds(pl.multiple_of(t * SR, SR), SR), :]
            for o in range(1, T):
                total = total + landing[o - 1, i]
            c = block(i)
            norms = row_norm * jnp.sqrt(sq_doc[c][0:1] + epsilon)
            out[:, pl.ds(pl.multiple_of(c * R, R), R)] = total / norms

    for b in wanted:
        finish(
            whole[b], got_z[b], send_z.at[b], recv_z.at[b], plan.count(b),
            lambda i, b=b: groups[b] * M + (column_member(g, groups[b], i) if b else i),
        )
    if plan.mirrored:
        for b in range(1, G):
            finish(
                mirror[b], got_mz[b], send_mz.at[b], recv_mz.at[b], H,
                lambda i, b=b: groups[b] * M + mirror_member(b, i),
            )

    for copy in pending:
        copy.wait_send()


def shards(doc_tiles, tile_list):
    D = lax.axis_size("doc")
    T = lax.axis_size("term")
    R, N, W = doc_tiles.shape
    plan = Plan(D, T, R, N, W)
    G, M, H, L, SR = plan.G, plan.M, plan.H, plan.L, plan.SR
    many = lambda *shape: pltpu.SemaphoreType.DMA(shape)
    buffer = lambda *shape: pltpu.VMEM(tuple(max(n, 1) for n in shape), jnp.float32)
    scratch = [pltpu.VMEM((M * (N + 1), R, L), doc_tiles.dtype) for _ in range(G)]
    scratch += [buffer(plan.count(a ^ b), R, R) for a in range(G) for b in range(G)]
    scratch += [buffer(plan.count(a ^ b), R, R) for a in range(1, G) for b in range(G)]
    scratch += [buffer(plan.count(b), R, R) for b in range(G)]
    scratch += [buffer(T - 1, plan.count(b), SR, R) for b in range(G)]
    if plan.mirrored:
        scratch += [buffer(H, R, R) for _ in range(1, G)]
        scratch += [buffer(H, R, R) for _ in range(1, G)]
        scratch += [buffer(T - 1, H, SR, R) for _ in range(1, G)]
    scratch += [pltpu.VMEM((R, N, L), doc_tiles.dtype) for _ in range(G)]
    scratch += [pltpu.VMEM((N, R, L), doc_tiles.dtype) for _ in range(1, G)]
    scratch += [buffer(T, 8, R), buffer(D, 8, R)]
    scratch += [pltpu.VMEM((G * D, LANES), jnp.int32), pltpu.SMEM((G * D, LANES), jnp.int32)]
    scratch += [
        many(G), pltpu.SemaphoreType.DMA,
        many(G, plan.parts), many(G, M, plan.parts), many(G, M, plan.parts),
        many(T), many(T), many(D), many(D),
        many(G, G), many(G, G), many(G, M), many(G, M),
        many(G, T), many(G, T), many(G, T), many(G, T),
    ]
    return pl.pallas_call(
        functools.partial(body, plan),
        out_shape=jax.ShapeDtypeStruct((SR, D * R), jnp.float32),
        in_specs=[
            pl.BlockSpec(memory_space=pltpu.VMEM),
            pl.BlockSpec(memory_space=pl.ANY),
        ],
        out_specs=pl.BlockSpec(memory_space=pltpu.VMEM),
        scratch_shapes=scratch,
        compiler_params=pltpu.CompilerParams(
            collective_id=0, has_side_effects=True, vmem_limit_bytes=56 * 1024 * 1024
        ),
        cost_estimate=pl.CostEstimate(
            flops=2 * G * R * D * R * N * L,
            bytes_accessed=R * N * W * 2 + SR * D * R * 4,
            transcendentals=0,
        ),
    )(tile_list, doc_tiles)


def solution(mesh):
    placed = (P("doc", None, "term"), P())
    return jax.shard_map(
        shards, mesh=mesh, in_specs=placed, out_specs=P(("doc", "term"), None), check_vma=False
    )
```

```python
import functools

import jax
import jax.numpy as jnp
from jax import lax
from jax.experimental import pallas as pl
from jax.experimental.pallas import tpu as pltpu
from jax.sharding import PartitionSpec as P

epsilon = 1e-06
LANES = 128
MESH = pl.DeviceIdType.MESH


def flip(g, o):
    bit = 1
    while bit <= o:
        if o & bit:
            g = g + bit - 2 * bit * lax.rem(lax.div(g, bit), 2)
        bit *= 2
    return g


class Plan:
    def __init__(self, D, T, R, N, W):
        G = 1
        while D % (2 * G) == 0 and W % (2 * G * LANES) == 0:
            G *= 2
        self.D, self.T, self.R, self.N, self.W, self.G = D, T, R, N, W, G
        self.M = D // G
        self.L = W // G
        self.SR = R // T
        self.mirrored = (
            G > 1 and self.M % 2 == 0 and R == LANES and self.SR % T == 0 and self.SR // T % 8 == 0
        )
        self.H = self.M // 2 if self.mirrored else self.M
        self.parts = 2 if N % 2 == 0 else 1
        self.step = N // self.parts
        self.rows = 16 if R % 16 == 0 else R

    def count(self, o):
        return self.M if o == 0 else self.H

    def wave(self, a, b):
        return 2 if max(self.stage(a), self.stage(b)) == 2 else 1

    def blocks(self, s, a):
        return [
            (b, i) for b in range(self.G) if self.wave(a, b) == s for i in range(self.count(a ^ b))
        ]

    def sets(self):
        return [(s, a) for s in (1, 2) for a in range(self.G) if self.blocks(s, a)]

    def stage(self, o):
        return 0 if o == 0 else 1 if o & (o - 1) == 0 else 2


def body(plan, names, docs, out, *scratch):
    D, T, G, M, H = plan.D, plan.T, plan.G, plan.M, plan.H
    R, N, L, SR = plan.R, plan.N, plan.L, plan.SR
    scratch = list(scratch)
    take = lambda n: [scratch.pop(0) for _ in range(n)]
    tiles = take(G)
    sets = plan.sets()
    part = {key: take(1)[0] for key in sets}
    got_z = {key: take(1)[0] for key in sets}
    mine = {key: take(1)[0] for key in sets}
    got_xy = {key: take(1)[0] for key in sets if key[1]}
    if plan.mirrored:
        turned = {b: take(1)[0] for b in range(1, G)}
        mirror = {b: take(1)[0] for b in range(1, G)}
    raw = take(G)
    ranges = [None] + take(G - 1)
    order, sq_term, sq_doc, table_rows, table = take(5)
    (
        raw_sem, table_sem, send_a, recv_a, send_f, send_st, recv_st, send_sd, recv_sd,
        send_p, recv_p, send_m, recv_m, send_z, recv_z,
    ) = scratch

    d = lax.axis_index("doc")
    t = lax.axis_index("term")
    g = lax.div(d, M)
    m = lax.rem(d, M)
    groups = [flip(g, o) for o in range(G)]

    def doc_peer(o):
        return lax.rem(d + o, D)

    def term_peer(o):
        return lax.rem(t + o, T)

    def sibling(i):
        return lax.rem(m + i, M)

    def remote(src, dst, ssem, rsem, doc, term):
        return pltpu.make_async_remote_copy(
            src_ref=src, dst_ref=dst, send_sem=ssem, recv_sem=rsem,
            device_id=(doc, term), device_id_type=MESH,
        )

    def column_member(row_group, column_group, i):
        if not plan.mirrored:
            return i
        return 2 * i + lax.rem(m + jnp.where(row_group < column_group, 1, 0), 2)

    parts, step = plan.parts, plan.step

    def slot(o, member, h):
        return tiles[o].at[pl.ds(member * (N + 1) + h * step, step)]

    def cut(group):
        if G == 1:
            return docs
        return docs.at[:, pl.ds(pl.multiple_of(group * L, L), L)]

    first = [o for o in range(1, G) if plan.stage(o) == 1]
    second = [o for o in range(1, G) if plan.stage(o) == 2]
    loads = {}
    for o in first + [0] + second:
        loads[o] = pltpu.make_async_copy(cut(groups[o]), raw[o], raw_sem.at[o])
        loads[o].start()

    barrier = pltpu.get_barrier_semaphore()
    greeted = [
        (o, u) for o in range(D) for u in range(T) if o + u and (plan.mirrored or not o * u)
    ]
    for o, u in greeted:
        pl.semaphore_signal(
            barrier, inc=1, device_id=(doc_peer(o), term_peer(u)), device_id_type=MESH
        )
    if greeted:
        pl.semaphore_wait(barrier, len(greeted))

    pending = []

    def begin(copy):
        copy.start()
        pending.append(copy)
        return copy

    def send_range(o, h):
        return begin(
            remote(
                ranges[o].at[pl.ds(h * step, step)], slot(o, m, h), send_a.at[o, h],
                recv_a.at[o, m, h], groups[o] * M + m, t,
            )
        )

    def hand_on(o, h):
        for i in range(1, M):
            begin(
                remote(
                    slot(o, m, h), slot(o, m, h), send_f.at[o, i, h], recv_a.at[o, m, h],
                    g * M + sibling(i), t,
                )
            )

    def take_over(o):
        for h in range(parts):
            for i in range(1, M):
                other = sibling(i)
                remote(
                    slot(o, other, h), slot(o, other, h), send_f.at[o, i, h], recv_a.at[o, other, h],
                    g * M + other, t,
                ).wait_recv()

    def arrived(o, h):
        remote(
            slot(o, m, h), slot(o, m, h), send_a.at[o, h], recv_a.at[o, m, h], groups[o] * M + m, t
        ).wait_recv()
        hand_on(o, h)

    def slots_first(o):
        loads[o].wait()

        def some_rows(k, carry):
            rows = pl.ds(pl.multiple_of(k * plan.rows, plan.rows), plan.rows)
            held = raw[o][pl.ds(pl.multiple_of(k * plan.rows * N, plan.rows * N), plan.rows * N), :]
            value = jnp.dot(order[...], held, preferred_element_type=jnp.float32)
            value = value.astype(docs.dtype).reshape(N, plan.rows, L)
            if o:
                ranges[o][:, rows, :] = value
            else:
                tiles[0][pl.ds(m * (N + 1), N), rows, :] = value
            return carry

        lax.fori_loop(0, R // plan.rows, some_rows, 0)

    size = plan.rows * N
    spot = lax.broadcasted_iota(jnp.int32, (size, size), 0)
    origin = lax.rem(spot, plan.rows) * N + lax.div(spot, plan.rows)
    hit = origin == lax.broadcasted_iota(jnp.int32, (size, size), 1)
    order[...] = jnp.where(hit, 1.0, 0.0).astype(docs.dtype)

    first_sends = []
    for o in first:
        slots_first(o)
        for h in range(parts):
            first_sends.append(send_range(o, h))
    slots_first(0)
    for h in range(parts):
        hand_on(0, h)
    for o in second:
        slots_first(o)
        for h in range(parts - 1):
            send_range(o, h)

    for o in range(G):
        tiles[o][m * (N + 1) + N] = jnp.zeros((R, L), docs.dtype)
    same = lax.broadcasted_iota(jnp.int32, (N, N), 0) == lax.broadcasted_iota(jnp.int32, (N, N), 1)
    place = lax.broadcasted_iota(jnp.int32, (N, N), 0)
    for a in range(G):
        line = names[pl.ds(groups[a] * M + m, 1), :]
        upright = jnp.sum(jnp.where(same, line, 0), axis=1, keepdims=True)
        for c in range(D):
            found = jnp.where(upright == names[c : c + 1, :], place, N)
            table_rows[a * D + c : a * D + c + 1, 0:N] = jnp.min(found, axis=0, keepdims=True)
    to_scalars = pltpu.make_async_copy(table_rows, table, table_sem)
    to_scalars.start()

    def add_square(a, total):
        for q in range(G):
            held = ranges[q][a] if q else tiles[0][m * (N + 1) + a]
            value = held.astype(jnp.float32)
            total = total + value * value
        return total

    square = lax.fori_loop(0, N, add_square, jnp.zeros((R, L), jnp.float32))
    column = jnp.sum(square, axis=1, keepdims=True)
    eye = lax.broadcasted_iota(jnp.int32, (R, R), 0) == lax.broadcasted_iota(jnp.int32, (R, R), 1)
    row = jnp.sum(jnp.where(eye, column, 0.0), axis=0, keepdims=True)
    sq_term[t] = jnp.broadcast_to(row, (8, R))
    for o in range(1, T):
        begin(remote(sq_term.at[t], sq_term.at[t], send_st.at[o], recv_st.at[t], d, term_peer(o)))
    for o in range(1, T):
        p = term_peer(o)
        remote(sq_term.at[p], sq_term.at[p], send_st.at[o], recv_st.at[p], d, p).wait_recv()
    total = sq_term[0]
    for q in range(1, T):
        total = total + sq_term[q]
    sq_doc[d] = total
    for o in range(1, D):
        begin(remote(sq_doc.at[d], sq_doc.at[d], send_sd.at[o], recv_sd.at[d], doc_peer(o), t))

    def pair(a, b):
        wave = plan.wave(a, b)
        base = plan.blocks(wave, a).index((b, 0))

        def one(i, carry):
            member = i if a == b else column_member(groups[a], groups[b], i)
            line = a * D + groups[b] * M + member
            left = jnp.concatenate(
                [tiles[a][m * (N + 1) + table[line, e]] for e in range(N)], axis=1
            )
            right = jnp.concatenate([tiles[b][member * (N + 1) + e] for e in range(N)], axis=1)
            part[wave, a][base + i] = lax.dot_general(
                left, right, (((1,), (1,)), ((), ())), preferred_element_type=jnp.float32
            )
            return carry

        number = plan.count(a ^ b)
        if number == 1:
            one(0, 0)
        else:
            lax.fori_loop(0, number, one, 0)

    wanted = list(range(1, G)) + [0]

    def pairs(wave, a):
        for b in range(G):
            if plan.wave(a, b) == wave:
                pair(a, b)

    def over_term(key):
        for o in range(1, T):
            p = term_peer(o)
            begin(
                remote(
                    part[key].at[:, pl.ds(p * SR, SR), :], got_z[key].at[o - 1],
                    send_z.at[key[0] - 1, key[1], o], recv_z.at[key[0] - 1, key[1], o], d, p,
                )
            )

    def sum_over_term(key):
        s, a = key
        for o in range(1, T):
            remote(
                part[key].at[:, pl.ds(t * SR, SR), :], got_z[key].at[o - 1],
                send_z.at[s - 1, a, o], recv_z.at[s - 1, a, o], d, term_peer(o),
            ).wait_recv()
        for i in range(len(plan.blocks(s, a))):
            total = part[key][i, pl.ds(pl.multiple_of(t * SR, SR), SR), :]
            for o in range(1, T):
                total = total + got_z[key][o - 1, i]
            mine[key][i] = total
        if a:
            begin(
                remote(
                    mine[key], got_xy[key], send_p.at[s - 1, a], recv_p.at[s - 1, a],
                    groups[a] * M + m, t,
                )
            )

    to_scalars.wait()
    take_over(0)
    for h in range(parts):
        for o in first:
            arrived(o, h)
    for copy in first_sends:
        copy.wait_send()
        pending.remove(copy)
    for o in second:
        send_range(o, parts - 1)
    for o in first:
        take_over(o)
    for a in wanted:
        if (1, a) in sets:
            pairs(1, a)
            over_term((1, a))
    for h in range(parts):
        for o in second:
            arrived(o, h)
    for o in second:
        take_over(o)
    for a in wanted:
        if (2, a) in sets:
            pairs(2, a)
            over_term((2, a))

    for key in sorted(sets, key=lambda key: (key[0], wanted.index(key[1]))):
        sum_over_term(key)
    for s, a in got_xy:
        remote(
            mine[s, a], got_xy[s, a], send_p.at[s - 1, a], recv_p.at[s - 1, a], groups[a] * M + m, t
        ).wait_recv()

    def mirror_member(b, i):
        return 2 * i + lax.rem(m + jnp.where(groups[b] < g, 1, 0), 2)

    lane_set = lax.div(lax.broadcasted_iota(jnp.int32, (max(SR // T, 1), R), 1), SR)
    sums = {}
    for b in wanted:
        for i in range(plan.count(b)):
            wave = plan.wave(0, b)
            total = mine[wave, 0][plan.blocks(wave, 0).index((b, i))]
            for a in range(1, G):
                wave = plan.wave(a, a ^ b)
                total = total + got_xy[wave, a][plan.blocks(wave, a).index((a ^ b, i))]
            sums[b, i] = total
            if plan.mirrored and b:
                upright = jnp.concatenate([total] * T, axis=0).T
                size = SR // T
                for u in range(T):
                    packed = jnp.zeros((size, R), jnp.float32)
                    for k in range(T):
                        lines = upright[u * SR + k * size : u * SR + (k + 1) * size]
                        packed = jnp.where(lane_set == k, lines, packed)
                    turned[b][i, u] = packed
                for w in range(T):
                    u = term_peer(w)
                    begin(
                        remote(
                            turned[b].at[i, u], mirror[b].at[lax.div(m, 2), t], send_m.at[b, i, w],
                            recv_m.at[b, lax.div(m, 2), t],
                            groups[b] * M + column_member(g, groups[b], i), u,
                        )
                    )

    for o in range(1, D):
        p = doc_peer(o)
        remote(sq_doc.at[p], sq_doc.at[p], send_sd.at[o], recv_sd.at[p], p, t).wait_recv()
    pick = lax.broadcasted_iota(jnp.int32, (SR, R), 1) == (
        lax.broadcasted_iota(jnp.int32, (SR, R), 0) + t * SR
    )
    own_column = jnp.sum(jnp.where(pick, sq_doc[d][0:1], 0.0), axis=1, keepdims=True)
    row_norm = jnp.sqrt(own_column + epsilon)

    def finish(total, c):
        norms = row_norm * jnp.sqrt(sq_doc[c][0:1] + epsilon)
        out[:, pl.ds(pl.multiple_of(c * R, R), R)] = total / norms

    for b, i in sums:
        finish(sums[b, i], groups[b] * M + (column_member(g, groups[b], i) if b else i))
    if plan.mirrored:
        for b in range(1, G):
            for i in range(H):
                c = groups[b] * M + mirror_member(b, i)
                for u in range(T):
                    remote(
                        turned[b].at[i, u], mirror[b].at[i, u], send_m.at[b, i, u],
                        recv_m.at[b, i, u], c, t,
                    ).wait_recv()
                lines = []
                for k in range(T):
                    line = jnp.zeros((SR // T, R), jnp.float32)
                    for u in range(T):
                        piece = mirror[b][i, u]
                        if u != k:
                            piece = pltpu.roll(piece, (u - k) % T * SR, 1)
                        line = jnp.where(lane_set == u, piece, line)
                    lines.append(line)
                finish(jnp.concatenate(lines, axis=0), c)

    for copy in pending:
        copy.wait_send()


def shards(doc_tiles, tile_list):
    D = lax.axis_size("doc")
    T = lax.axis_size("term")
    R, N, W = doc_tiles.shape
    plan = Plan(D, T, R, N, W)
    G, M, H, L, SR = plan.G, plan.M, plan.H, plan.L, plan.SR
    many = lambda *shape: pltpu.SemaphoreType.DMA(shape)
    buffer = lambda *shape: pltpu.VMEM(tuple(max(n, 1) for n in shape), jnp.float32)
    scratch = [pltpu.VMEM((M * (N + 1), R, L), doc_tiles.dtype) for _ in range(G)]
    numbers = [len(plan.blocks(*key)) for key in plan.sets()]
    scratch += [buffer(n, R, R) for n in numbers]
    scratch += [buffer(T - 1, n, SR, R) for n in numbers]
    scratch += [buffer(n, SR, R) for n in numbers]
    scratch += [buffer(len(plan.blocks(s, a)), SR, R) for s, a in plan.sets() if a]
    if plan.mirrored:
        scratch += [buffer(H, T, SR // T, R) for _ in range(1, G)]
        scratch += [buffer(H, T, SR // T, R) for _ in range(1, G)]
    scratch += [pltpu.VMEM((R * N, L), doc_tiles.dtype) for _ in range(G)]
    scratch += [pltpu.VMEM((N, R, L), doc_tiles.dtype) for _ in range(1, G)]
    scratch += [pltpu.VMEM((plan.rows * N, plan.rows * N), doc_tiles.dtype)]
    scratch += [buffer(T, 8, R), buffer(D, 8, R)]
    scratch += [pltpu.VMEM((G * D, LANES), jnp.int32), pltpu.SMEM((G * D, LANES), jnp.int32)]
    scratch += [
        many(G), pltpu.SemaphoreType.DMA,
        many(G, plan.parts), many(G, M, plan.parts), many(G, M, plan.parts),
        many(T), many(T), many(D), many(D),
        many(2, G), many(2, G), many(G, M, T), many(G, M, T),
        many(2, G, T), many(2, G, T),
    ]
    return pl.pallas_call(
        functools.partial(body, plan),
        out_shape=jax.ShapeDtypeStruct((SR, D * R), jnp.float32),
        in_specs=[
            pl.BlockSpec(memory_space=pltpu.VMEM),
            pl.BlockSpec(memory_space=pl.ANY),
        ],
        out_specs=pl.BlockSpec(memory_space=pltpu.VMEM),
        scratch_shapes=scratch,
        compiler_params=pltpu.CompilerParams(
            collective_id=0, has_side_effects=True, vmem_limit_bytes=56 * 1024 * 1024
        ),
        cost_estimate=pl.CostEstimate(
            flops=2 * G * R * D * R * N * L,
            bytes_accessed=R * N * W * 2 + SR * D * R * 4,
            transcendentals=0,
        ),
    )(tile_list, doc_tiles.reshape(R * N, W))


def solution(mesh):
    placed = (P("doc", None, "term"), P())
    return jax.shard_map(
        shards, mesh=mesh, in_specs=placed, out_specs=P(("doc", "term"), None), check_vma=False
    )
```

```python
import functools

import jax
import jax.numpy as jnp
from jax import lax
from jax.experimental import pallas as pl
from jax.experimental.pallas import tpu as pltpu
from jax.sharding import PartitionSpec as P

epsilon = 1e-06
LANES = 128
MESH = pl.DeviceIdType.MESH


def flip(g, o):
    bit = 1
    while bit <= o:
        if o & bit:
            g = g + bit - 2 * bit * lax.rem(lax.div(g, bit), 2)
        bit *= 2
    return g


class Plan:
    def __init__(self, D, T, R, N, W):
        G = 1
        while D % (2 * G) == 0 and W % (2 * G * LANES) == 0:
            G *= 2
        self.D, self.T, self.R, self.N, self.W, self.G = D, T, R, N, W, G
        self.M = D // G
        self.L = W // G
        self.SR = R // T
        self.mirrored = (
            G > 1 and self.M % 2 == 0 and R == LANES and self.SR % T == 0 and self.SR // T % 8 == 0
        )
        self.H = self.M // 2 if self.mirrored else self.M
        self.parts = 2 if N % 2 == 0 else 1
        self.step = N // self.parts
        self.rows = 16 if R % 16 == 0 else R

    def count(self, o):
        return self.M if o == 0 else self.H

    def stage(self, o):
        return 0 if o == 0 else 1 if o & (o - 1) == 0 else 2


def body(plan, names, docs, out, *scratch):
    D, T, G, M, H = plan.D, plan.T, plan.G, plan.M, plan.H
    R, N, L, SR = plan.R, plan.N, plan.L, plan.SR
    scratch = list(scratch)
    take = lambda n: [scratch.pop(0) for _ in range(n)]
    tiles = take(G)
    part = {(a, b): take(1)[0] for a in range(G) for b in range(G)}
    got = {(a, b): take(1)[0] for a in range(1, G) for b in range(G)}
    whole = {b: take(1)[0] for b in range(G)}
    got_z = {b: take(1)[0] for b in range(G)}
    if plan.mirrored:
        turned = {b: take(1)[0] for b in range(1, G)}
        mirror = {b: take(1)[0] for b in range(1, G)}
    raw = take(G)
    ranges = [None] + take(G - 1)
    order, sq_term, sq_doc, table_rows, table = take(5)
    (
        raw_sem, table_sem, send_a, recv_a, send_f, send_st, recv_st, send_sd, recv_sd,
        send_p, recv_p, send_m, recv_m, send_z, recv_z,
    ) = scratch

    d = lax.axis_index("doc")
    t = lax.axis_index("term")
    g = lax.div(d, M)
    m = lax.rem(d, M)
    groups = [flip(g, o) for o in range(G)]

    def doc_peer(o):
        return lax.rem(d + o, D)

    def term_peer(o):
        return lax.rem(t + o, T)

    def sibling(i):
        return lax.rem(m + i, M)

    def remote(src, dst, ssem, rsem, doc, term):
        return pltpu.make_async_remote_copy(
            src_ref=src, dst_ref=dst, send_sem=ssem, recv_sem=rsem,
            device_id=(doc, term), device_id_type=MESH,
        )

    def column_member(row_group, column_group, i):
        if not plan.mirrored:
            return i
        return 2 * i + lax.rem(m + jnp.where(row_group < column_group, 1, 0), 2)

    parts, step = plan.parts, plan.step

    def slot(o, member, h):
        return tiles[o].at[pl.ds(member * (N + 1) + h * step, step)]

    def cut(group):
        if G == 1:
            return docs
        return docs.at[:, pl.ds(pl.multiple_of(group * L, L), L)]

    first = [o for o in range(1, G) if plan.stage(o) == 1]
    second = [o for o in range(1, G) if plan.stage(o) == 2]
    loads = {}
    for o in first + [0] + second:
        loads[o] = pltpu.make_async_copy(cut(groups[o]), raw[o], raw_sem.at[o])
        loads[o].start()

    barrier = pltpu.get_barrier_semaphore()
    greeted = [
        (o, u) for o in range(D) for u in range(T) if o + u and (plan.mirrored or not o * u)
    ]
    for o, u in greeted:
        pl.semaphore_signal(
            barrier, inc=1, device_id=(doc_peer(o), term_peer(u)), device_id_type=MESH
        )
    if greeted:
        pl.semaphore_wait(barrier, len(greeted))

    pending = []

    def begin(copy):
        copy.start()
        pending.append(copy)
        return copy

    def send_range(o, h):
        return begin(
            remote(
                ranges[o].at[pl.ds(h * step, step)], slot(o, m, h), send_a.at[o, h],
                recv_a.at[o, m, h], groups[o] * M + m, t,
            )
        )

    def hand_on(o, h):
        for i in range(1, M):
            begin(
                remote(
                    slot(o, m, h), slot(o, m, h), send_f.at[o, i, h], recv_a.at[o, m, h],
                    g * M + sibling(i), t,
                )
            )

    def take_over(o):
        for h in range(parts):
            for i in range(1, M):
                other = sibling(i)
                remote(
                    slot(o, other, h), slot(o, other, h), send_f.at[o, i, h], recv_a.at[o, other, h],
                    g * M + other, t,
                ).wait_recv()

    def arrived(o, h):
        remote(
            slot(o, m, h), slot(o, m, h), send_a.at[o, h], recv_a.at[o, m, h], groups[o] * M + m, t
        ).wait_recv()
        hand_on(o, h)

    def slots_first(o):
        loads[o].wait()

        def some_rows(k, carry):
            rows = pl.ds(pl.multiple_of(k * plan.rows, plan.rows), plan.rows)
            held = raw[o][pl.ds(pl.multiple_of(k * plan.rows * N, plan.rows * N), plan.rows * N), :]
            value = jnp.dot(order[...], held, preferred_element_type=jnp.float32)
            value = value.astype(docs.dtype).reshape(N, plan.rows, L)
            if o:
                ranges[o][:, rows, :] = value
            else:
                tiles[0][pl.ds(m * (N + 1), N), rows, :] = value
            return carry

        lax.fori_loop(0, R // plan.rows, some_rows, 0)

    size = plan.rows * N
    spot = lax.broadcasted_iota(jnp.int32, (size, size), 0)
    origin = lax.rem(spot, plan.rows) * N + lax.div(spot, plan.rows)
    hit = origin == lax.broadcasted_iota(jnp.int32, (size, size), 1)
    order[...] = jnp.where(hit, 1.0, 0.0).astype(docs.dtype)

    first_sends = []
    for o in first:
        slots_first(o)
        for h in range(parts):
            first_sends.append(send_range(o, h))
    slots_first(0)
    for h in range(parts):
        hand_on(0, h)
    for o in second:
        slots_first(o)
        for h in range(parts - 1):
            send_range(o, h)

    for o in range(G):
        tiles[o][m * (N + 1) + N] = jnp.zeros((R, L), docs.dtype)
    same = lax.broadcasted_iota(jnp.int32, (N, N), 0) == lax.broadcasted_iota(jnp.int32, (N, N), 1)
    place = lax.broadcasted_iota(jnp.int32, (N, N), 0)
    for a in range(G):
        line = names[pl.ds(groups[a] * M + m, 1), :]
        upright = jnp.sum(jnp.where(same, line, 0), axis=1, keepdims=True)
        for c in range(D):
            found = jnp.where(upright == names[c : c + 1, :], place, N)
            table_rows[a * D + c : a * D + c + 1, 0:N] = jnp.min(found, axis=0, keepdims=True)
    to_scalars = pltpu.make_async_copy(table_rows, table, table_sem)
    to_scalars.start()

    def add_square(a, total):
        for q in range(G):
            held = ranges[q][a] if q else tiles[0][m * (N + 1) + a]
            value = held.astype(jnp.float32)
            total = total + value * value
        return total

    square = lax.fori_loop(0, N, add_square, jnp.zeros((R, L), jnp.float32))
    column = jnp.sum(square, axis=1, keepdims=True)
    eye = lax.broadcasted_iota(jnp.int32, (R, R), 0) == lax.broadcasted_iota(jnp.int32, (R, R), 1)
    row = jnp.sum(jnp.where(eye, column, 0.0), axis=0, keepdims=True)
    sq_term[t] = jnp.broadcast_to(row, (8, R))
    for o in range(1, T):
        begin(remote(sq_term.at[t], sq_term.at[t], send_st.at[o], recv_st.at[t], d, term_peer(o)))
    for o in range(1, T):
        p = term_peer(o)
        remote(sq_term.at[p], sq_term.at[p], send_st.at[o], recv_st.at[p], d, p).wait_recv()
    total = sq_term[0]
    for q in range(1, T):
        total = total + sq_term[q]
    sq_doc[d] = total
    for o in range(1, D):
        begin(remote(sq_doc.at[d], sq_doc.at[d], send_sd.at[o], recv_sd.at[d], doc_peer(o), t))

    def pair(a, b):
        def one(i, carry):
            member = i if a == b else column_member(groups[a], groups[b], i)
            line = a * D + groups[b] * M + member
            left = jnp.concatenate(
                [tiles[a][m * (N + 1) + table[line, e]] for e in range(N)], axis=1
            )
            right = jnp.concatenate([tiles[b][member * (N + 1) + e] for e in range(N)], axis=1)
            part[a, b][i] = lax.dot_general(
                left, right, (((1,), (1,)), ((), ())), preferred_element_type=jnp.float32
            )
            return carry

        number = plan.count(a ^ b)
        if number == 1:
            one(0, 0)
        else:
            lax.fori_loop(0, number, one, 0)
        if a:
            begin(
                remote(
                    part[a, b], got[a, b], send_p.at[a, b], recv_p.at[a, b], groups[a] * M + m, t
                )
            )

    wanted = list(range(1, G)) + [0]

    def pairs(stage):
        todo = [
            (a, b)
            for a in range(G)
            for b in range(G)
            if max(plan.stage(a), plan.stage(b)) == stage
        ]
        for a, b in sorted(todo, key=lambda ab: (wanted.index(ab[0] ^ ab[1]), -ab[0])):
            pair(a, b)

    to_scalars.wait()
    take_over(0)
    pairs(0)
    for h in range(parts):
        for o in first:
            arrived(o, h)
    for copy in first_sends:
        copy.wait_send()
        pending.remove(copy)
    for o in second:
        send_range(o, parts - 1)
    for o in first:
        take_over(o)
    if first:
        pairs(1)
    for h in range(parts):
        for o in second:
            arrived(o, h)
    for o in second:
        take_over(o)
    if second:
        pairs(2)

    def over_term(source, landing, ssem, rsem):
        for o in range(1, T):
            p = term_peer(o)
            begin(
                remote(
                    source.at[:, pl.ds(p * SR, SR), :], landing.at[o - 1], ssem.at[o], rsem.at[o], d, p
                )
            )

    for b in wanted:
        for a in range(1, G):
            remote(
                part[a, a ^ b], got[a, a ^ b], send_p.at[a, a ^ b], recv_p.at[a, a ^ b],
                groups[a] * M + m, t,
            ).wait_recv()
        for i in range(plan.count(b)):
            total = part[0, b][i]
            for a in range(1, G):
                total = total + got[a, a ^ b][i]
            whole[b][i] = total
        over_term(whole[b], got_z[b], send_z.at[b], recv_z.at[b])

    def mirror_member(b, i):
        return 2 * i + lax.rem(m + jnp.where(groups[b] < g, 1, 0), 2)

    lane_set = lax.div(lax.broadcasted_iota(jnp.int32, (max(SR // T, 1), R), 1), SR)
    sums = {}
    for b in wanted:
        for o in range(1, T):
            remote(
                whole[b].at[:, pl.ds(t * SR, SR), :], got_z[b].at[o - 1], send_z.at[b, o],
                recv_z.at[b, o], d, term_peer(o),
            ).wait_recv()
        for i in range(plan.count(b)):
            total = whole[b][i, pl.ds(pl.multiple_of(t * SR, SR), SR), :]
            for o in range(1, T):
                total = total + got_z[b][o - 1, i]
            sums[b, i] = total
            if plan.mirrored and b:
                upright = jnp.concatenate([total] * T, axis=0).T
                size = SR // T
                for u in range(T):
                    packed = jnp.zeros((size, R), jnp.float32)
                    for k in range(T):
                        lines = upright[u * SR + k * size : u * SR + (k + 1) * size]
                        packed = jnp.where(lane_set == k, lines, packed)
                    turned[b][i, u] = packed
                for w in range(T):
                    u = term_peer(w)
                    begin(
                        remote(
                            turned[b].at[i, u], mirror[b].at[lax.div(m, 2), t], send_m.at[b, i, w],
                            recv_m.at[b, lax.div(m, 2), t],
                            groups[b] * M + column_member(g, groups[b], i), u,
                        )
                    )

    for o in range(1, D):
        p = doc_peer(o)
        remote(sq_doc.at[p], sq_doc.at[p], send_sd.at[o], recv_sd.at[p], p, t).wait_recv()
    pick = lax.broadcasted_iota(jnp.int32, (SR, R), 1) == (
        lax.broadcasted_iota(jnp.int32, (SR, R), 0) + t * SR
    )
    own_column = jnp.sum(jnp.where(pick, sq_doc[d][0:1], 0.0), axis=1, keepdims=True)
    row_norm = jnp.sqrt(own_column + epsilon)

    def finish(total, c):
        norms = row_norm * jnp.sqrt(sq_doc[c][0:1] + epsilon)
        out[:, pl.ds(pl.multiple_of(c * R, R), R)] = total / norms

    for b, i in sums:
        finish(sums[b, i], groups[b] * M + (column_member(g, groups[b], i) if b else i))
    if plan.mirrored:
        for b in range(1, G):
            for i in range(H):
                c = groups[b] * M + mirror_member(b, i)
                for u in range(T):
                    remote(
                        turned[b].at[i, u], mirror[b].at[i, u], send_m.at[b, i, u],
                        recv_m.at[b, i, u], c, t,
                    ).wait_recv()
                lines = []
                for k in range(T):
                    line = jnp.zeros((SR // T, R), jnp.float32)
                    for u in range(T):
                        piece = mirror[b][i, u]
                        if u != k:
                            piece = pltpu.roll(piece, (u - k) % T * SR, 1)
                        line = jnp.where(lane_set == u, piece, line)
                    lines.append(line)
                finish(jnp.concatenate(lines, axis=0), c)

    for copy in pending:
        copy.wait_send()


def shards(doc_tiles, tile_list):
    D = lax.axis_size("doc")
    T = lax.axis_size("term")
    R, N, W = doc_tiles.shape
    plan = Plan(D, T, R, N, W)
    G, M, H, L, SR = plan.G, plan.M, plan.H, plan.L, plan.SR
    many = lambda *shape: pltpu.SemaphoreType.DMA(shape)
    buffer = lambda *shape: pltpu.VMEM(tuple(max(n, 1) for n in shape), jnp.float32)
    scratch = [pltpu.VMEM((M * (N + 1), R, L), doc_tiles.dtype) for _ in range(G)]
    scratch += [buffer(plan.count(a ^ b), R, R) for a in range(G) for b in range(G)]
    scratch += [buffer(plan.count(a ^ b), R, R) for a in range(1, G) for b in range(G)]
    scratch += [buffer(plan.count(b), R, R) for b in range(G)]
    scratch += [buffer(T - 1, plan.count(b), SR, R) for b in range(G)]
    if plan.mirrored:
        scratch += [buffer(H, T, SR // T, R) for _ in range(1, G)]
        scratch += [buffer(H, T, SR // T, R) for _ in range(1, G)]
    scratch += [pltpu.VMEM((R * N, L), doc_tiles.dtype) for _ in range(G)]
    scratch += [pltpu.VMEM((N, R, L), doc_tiles.dtype) for _ in range(1, G)]
    scratch += [pltpu.VMEM((plan.rows * N, plan.rows * N), doc_tiles.dtype)]
    scratch += [buffer(T, 8, R), buffer(D, 8, R)]
    scratch += [pltpu.VMEM((G * D, LANES), jnp.int32), pltpu.SMEM((G * D, LANES), jnp.int32)]
    scratch += [
        many(G), pltpu.SemaphoreType.DMA,
        many(G, plan.parts), many(G, M, plan.parts), many(G, M, plan.parts),
        many(T), many(T), many(D), many(D),
        many(G, G), many(G, G), many(G, M, T), many(G, M, T),
        many(G, T), many(G, T),
    ]
    return pl.pallas_call(
        functools.partial(body, plan),
        out_shape=jax.ShapeDtypeStruct((SR, D * R), jnp.float32),
        in_specs=[
            pl.BlockSpec(memory_space=pltpu.VMEM),
            pl.BlockSpec(memory_space=pl.ANY),
        ],
        out_specs=pl.BlockSpec(memory_space=pltpu.VMEM),
        scratch_shapes=scratch,
        compiler_params=pltpu.CompilerParams(
            collective_id=0, has_side_effects=True, vmem_limit_bytes=56 * 1024 * 1024
        ),
        cost_estimate=pl.CostEstimate(
            flops=2 * G * R * D * R * N * L,
            bytes_accessed=R * N * W * 2 + SR * D * R * 4,
            transcendentals=0,
        ),
    )(tile_list, doc_tiles.reshape(R * N, W))


def solution(mesh):
    placed = (P("doc", None, "term"), P())
    return jax.shard_map(
        shards, mesh=mesh, in_specs=placed, out_specs=P(("doc", "term"), None), check_vma=False
    )
```

```python
import functools

import jax
import jax.numpy as jnp
from jax import lax
from jax.experimental import pallas as pl
from jax.experimental.pallas import tpu as pltpu
from jax.sharding import PartitionSpec as P

epsilon = 1e-06
LANES = 128
MESH = pl.DeviceIdType.MESH


def flip(g, o):
    bit = 1
    while bit <= o:
        if o & bit:
            g = g + bit - 2 * bit * lax.rem(lax.div(g, bit), 2)
        bit *= 2
    return g


class Plan:
    def __init__(self, D, T, R, N, W):
        G = 1
        while D % (2 * G) == 0 and W % (2 * G * LANES) == 0:
            G *= 2
        self.D, self.T, self.R, self.N, self.W, self.G = D, T, R, N, W, G
        self.M = D // G
        self.L = W // G
        self.SR = R // T
        self.mirrored = (
            G > 1 and self.M % 2 == 0 and R == LANES and self.SR % T == 0 and self.SR // T % 8 == 0
        )
        self.H = self.M // 2 if self.mirrored else self.M
        self.parts = 2 if N % 2 == 0 else 1
        self.step = N // self.parts
        self.rows = 16 if R % 16 == 0 else R

    def count(self, o):
        return self.M if o == 0 else self.H

    def wave(self, a, b):
        return max(self.stage(a), self.stage(b))

    def term_first(self, a, b):
        return a > 0 and (self.wave(a, b) == 1 or a == b)

    def blocks(self, wave, a):
        return [
            (b, i)
            for b in range(self.G)
            if self.wave(a, b) == wave and self.term_first(a, b)
            for i in range(self.count(a ^ b))
        ]

    def sets(self):
        return [(w, a) for w in (1, 2) for a in range(1, self.G) if self.blocks(w, a)]

    def direct(self):
        return [
            (a, b) for a in range(self.G) for b in range(self.G) if not self.term_first(a, b)
        ]

    def stage(self, o):
        return 0 if o == 0 else 1 if o & (o - 1) == 0 else 2


def body(plan, names, docs, out, *scratch):
    D, T, G, M, H = plan.D, plan.T, plan.G, plan.M, plan.H
    R, N, L, SR = plan.R, plan.N, plan.L, plan.SR
    scratch = list(scratch)
    take = lambda n: [scratch.pop(0) for _ in range(n)]
    tiles = take(G)
    part = {pair: take(1)[0] for pair in plan.direct()}
    got = {pair: take(1)[0] for pair in plan.direct() if pair[0]}
    early = {key: take(1)[0] for key in plan.sets()}
    early_z = {key: take(1)[0] for key in plan.sets()}
    early_sum = {key: take(1)[0] for key in plan.sets()}
    early_xy = {key: take(1)[0] for key in plan.sets()}
    whole = {b: take(1)[0] for b in range(G)}
    got_z = {b: take(1)[0] for b in range(G)}
    if plan.mirrored:
        turned = {b: take(1)[0] for b in range(1, G)}
        mirror = {b: take(1)[0] for b in range(1, G)}
    raw = take(G)
    ranges = [None] + take(G - 1)
    order, sq_term, sq_doc, table_rows, table = take(5)
    (
        raw_sem, table_sem, send_a, recv_a, send_f, send_st, recv_st, send_sd, recv_sd,
        send_p, recv_p, send_m, recv_m, send_z, recv_z, send_ez, recv_ez, send_ex, recv_ex,
    ) = scratch

    d = lax.axis_index("doc")
    t = lax.axis_index("term")
    g = lax.div(d, M)
    m = lax.rem(d, M)
    groups = [flip(g, o) for o in range(G)]

    def doc_peer(o):
        return lax.rem(d + o, D)

    def term_peer(o):
        return lax.rem(t + o, T)

    def sibling(i):
        return lax.rem(m + i, M)

    def remote(src, dst, ssem, rsem, doc, term):
        return pltpu.make_async_remote_copy(
            src_ref=src, dst_ref=dst, send_sem=ssem, recv_sem=rsem,
            device_id=(doc, term), device_id_type=MESH,
        )

    def column_member(row_group, column_group, i):
        if not plan.mirrored:
            return i
        return 2 * i + lax.rem(m + jnp.where(row_group < column_group, 1, 0), 2)

    parts, step = plan.parts, plan.step

    def slot(o, member, h):
        return tiles[o].at[pl.ds(member * (N + 1) + h * step, step)]

    def cut(group):
        if G == 1:
            return docs
        return docs.at[:, pl.ds(pl.multiple_of(group * L, L), L)]

    first = [o for o in range(1, G) if plan.stage(o) == 1]
    second = [o for o in range(1, G) if plan.stage(o) == 2]
    loads = {}
    for o in first + [0] + second:
        loads[o] = pltpu.make_async_copy(cut(groups[o]), raw[o], raw_sem.at[o])
        loads[o].start()

    barrier = pltpu.get_barrier_semaphore()
    greeted = [
        (o, u) for o in range(D) for u in range(T) if o + u and (plan.mirrored or not o * u)
    ]
    for o, u in greeted:
        pl.semaphore_signal(
            barrier, inc=1, device_id=(doc_peer(o), term_peer(u)), device_id_type=MESH
        )
    pending = []

    def begin(copy):
        copy.start()
        pending.append(copy)
        return copy

    def send_range(o, h):
        return begin(
            remote(
                ranges[o].at[pl.ds(h * step, step)], slot(o, m, h), send_a.at[o, h],
                recv_a.at[o, m, h], groups[o] * M + m, t,
            )
        )

    def hand_on(o, h):
        for i in range(1, M):
            begin(
                remote(
                    slot(o, m, h), slot(o, m, h), send_f.at[o, i, h], recv_a.at[o, m, h],
                    g * M + sibling(i), t,
                )
            )

    def take_over(o):
        for h in range(parts):
            for i in range(1, M):
                other = sibling(i)
                remote(
                    slot(o, other, h), slot(o, other, h), send_f.at[o, i, h], recv_a.at[o, other, h],
                    g * M + other, t,
                ).wait_recv()

    def arrived(o, h):
        remote(
            slot(o, m, h), slot(o, m, h), send_a.at[o, h], recv_a.at[o, m, h], groups[o] * M + m, t
        ).wait_recv()
        hand_on(o, h)

    def slots_first(o):
        loads[o].wait()

        def some_rows(k, carry):
            rows = pl.ds(pl.multiple_of(k * plan.rows, plan.rows), plan.rows)
            held = raw[o][pl.ds(pl.multiple_of(k * plan.rows * N, plan.rows * N), plan.rows * N), :]
            value = jnp.dot(order[...], held, preferred_element_type=jnp.float32)
            value = value.astype(docs.dtype).reshape(N, plan.rows, L)
            if o:
                ranges[o][:, rows, :] = value
            else:
                tiles[0][pl.ds(m * (N + 1), N), rows, :] = value
            return carry

        lax.fori_loop(0, R // plan.rows, some_rows, 0)

    size = plan.rows * N
    origin = jnp.concatenate(
        [lax.broadcasted_iota(jnp.int32, (plan.rows, 1), 0) * N + a for a in range(N)], axis=0
    )
    hit = origin == lax.broadcasted_iota(jnp.int32, (size, size), 1)
    order[...] = jnp.where(hit, 1.0, 0.0).astype(docs.dtype)

    first_sends = []
    if first:
        slots_first(first[0])
    if greeted:
        pl.semaphore_wait(barrier, len(greeted))
    for o in first:
        if o != first[0]:
            slots_first(o)
        for h in range(parts):
            first_sends.append(send_range(o, h))
    slots_first(0)
    for h in range(parts):
        hand_on(0, h)
    for o in second:
        slots_first(o)
        for h in range(parts - 1):
            send_range(o, h)

    for o in range(G):
        tiles[o][m * (N + 1) + N] = jnp.zeros((R, L), docs.dtype)
    same = lax.broadcasted_iota(jnp.int32, (N, N), 0) == lax.broadcasted_iota(jnp.int32, (N, N), 1)
    place = lax.broadcasted_iota(jnp.int32, (N, N), 0)
    for a in range(G):
        line = names[pl.ds(groups[a] * M + m, 1), :]
        upright = jnp.sum(jnp.where(same, line, 0), axis=1, keepdims=True)
        for c in range(D):
            found = jnp.where(upright == names[c : c + 1, :], place, N)
            table_rows[a * D + c : a * D + c + 1, 0:N] = jnp.min(found, axis=0, keepdims=True)
    to_scalars = pltpu.make_async_copy(table_rows, table, table_sem)
    to_scalars.start()

    def add_square(a, total):
        for q in range(G):
            held = ranges[q][a] if q else tiles[0][m * (N + 1) + a]
            value = held.astype(jnp.float32)
            total = total + value * value
        return total

    square = lax.fori_loop(0, N, add_square, jnp.zeros((R, L), jnp.float32))
    column = jnp.sum(square, axis=1, keepdims=True)
    eye = lax.broadcasted_iota(jnp.int32, (R, R), 0) == lax.broadcasted_iota(jnp.int32, (R, R), 1)
    row = jnp.sum(jnp.where(eye, column, 0.0), axis=0, keepdims=True)
    sq_term[t] = jnp.broadcast_to(row, (8, R))
    for o in range(1, T):
        begin(remote(sq_term.at[t], sq_term.at[t], send_st.at[o], recv_st.at[t], d, term_peer(o)))
    for o in range(1, T):
        p = term_peer(o)
        remote(sq_term.at[p], sq_term.at[p], send_st.at[o], recv_st.at[p], d, p).wait_recv()
    total = sq_term[0]
    for q in range(1, T):
        total = total + sq_term[q]
    sq_doc[d] = total
    for o in range(1, D):
        begin(remote(sq_doc.at[d], sq_doc.at[d], send_sd.at[o], recv_sd.at[d], doc_peer(o), t))

    def over_term(source, landing, ssem, rsem):
        for o in range(1, T):
            p = term_peer(o)
            begin(
                remote(
                    source.at[:, pl.ds(p * SR, SR), :], landing.at[o - 1], ssem.at[o], rsem.at[o], d, p
                )
            )

    def pair(a, b):
        wave = plan.wave(a, b)
        if plan.term_first(a, b):
            target, base = early[wave, a], plan.blocks(wave, a).index((b, 0))
        else:
            target, base = part[a, b], 0

        def one(i, carry):
            member = i if a == b else column_member(groups[a], groups[b], i)
            line = a * D + groups[b] * M + member
            left = jnp.concatenate(
                [tiles[a][m * (N + 1) + table[line, e]] for e in range(N)], axis=1
            )
            right = jnp.concatenate([tiles[b][member * (N + 1) + e] for e in range(N)], axis=1)
            target[base + i] = lax.dot_general(
                left, right, (((1,), (1,)), ((), ())), preferred_element_type=jnp.float32
            )
            return carry

        number = plan.count(a ^ b)
        if number == 1:
            one(0, 0)
        else:
            lax.fori_loop(0, number, one, 0)
        if plan.term_first(a, b):
            if plan.blocks(wave, a)[-1][0] == b:
                over_term(
                    early[wave, a], early_z[wave, a], send_ez.at[wave - 1, a], recv_ez.at[wave - 1, a]
                )
        elif a:
            begin(
                remote(
                    part[a, b], got[a, b], send_p.at[a, b], recv_p.at[a, b], groups[a] * M + m, t
                )
            )

    wanted = list(range(1, G)) + [0]

    def pairs(stage):
        todo = [
            (a, b)
            for a in range(G)
            for b in range(G)
            if plan.wave(a, b) == stage
        ]
        for a, b in [p for p in todo if plan.term_first(*p)]:
            pair(a, b)
        rest = [p for p in todo if not plan.term_first(*p)]
        for a, b in sorted(rest, key=lambda ab: (wanted.index(ab[0] ^ ab[1]), -ab[0])):
            pair(a, b)

    to_scalars.wait()
    take_over(0)
    pairs(0)
    for h in range(parts):
        for o in first:
            arrived(o, h)
    for copy in first_sends:
        copy.wait_send()
        pending.remove(copy)
    for o in second:
        send_range(o, parts - 1)
    for o in first:
        take_over(o)
    if first:
        pairs(1)
    for h in range(parts):
        for o in second:
            arrived(o, h)
    for o in second:
        take_over(o)
    if second:
        pairs(2)

    def pass_early(wave):
        for w, a in [key for key in plan.sets() if key[0] == wave]:
            for o in range(1, T):
                remote(
                    early[w, a].at[:, pl.ds(t * SR, SR), :], early_z[w, a].at[o - 1],
                    send_ez.at[w - 1, a, o], recv_ez.at[w - 1, a, o], d, term_peer(o),
                ).wait_recv()
            for i in range(len(plan.blocks(w, a))):
                total = early[w, a][i, pl.ds(pl.multiple_of(t * SR, SR), SR), :]
                for o in range(1, T):
                    total = total + early_z[w, a][o - 1, i]
                early_sum[w, a][i] = total
            begin(
                remote(
                    early_sum[w, a], early_xy[w, a], send_ex.at[w - 1, a], recv_ex.at[w - 1, a],
                    groups[a] * M + m, t,
                )
            )

    pass_early(1)
    for b in wanted:
        direct = [a for a in range(1, G) if not plan.term_first(a, a ^ b)]
        for a in direct:
            remote(
                part[a, a ^ b], got[a, a ^ b], send_p.at[a, a ^ b], recv_p.at[a, a ^ b],
                groups[a] * M + m, t,
            ).wait_recv()
        for i in range(plan.count(b)):
            total = part[0, b][i]
            for a in direct:
                total = total + got[a, a ^ b][i]
            whole[b][i] = total
        over_term(whole[b], got_z[b], send_z.at[b], recv_z.at[b])
    pass_early(2)

    def mirror_member(b, i):
        return 2 * i + lax.rem(m + jnp.where(groups[b] < g, 1, 0), 2)

    lane_set = lax.div(lax.broadcasted_iota(jnp.int32, (max(SR // T, 1), R), 1), SR)
    for w, a in plan.sets():
        remote(
            early_sum[w, a], early_xy[w, a], send_ex.at[w - 1, a], recv_ex.at[w - 1, a],
            groups[a] * M + m, t,
        ).wait_recv()
    sums = {}
    for b in wanted:
        for o in range(1, T):
            remote(
                whole[b].at[:, pl.ds(t * SR, SR), :], got_z[b].at[o - 1], send_z.at[b, o],
                recv_z.at[b, o], d, term_peer(o),
            ).wait_recv()
        for i in range(plan.count(b)):
            total = whole[b][i, pl.ds(pl.multiple_of(t * SR, SR), SR), :]
            for o in range(1, T):
                total = total + got_z[b][o - 1, i]
            for a in range(1, G):
                if plan.term_first(a, a ^ b):
                    wave = plan.wave(a, a ^ b)
                    total = total + early_xy[wave, a][plan.blocks(wave, a).index((a ^ b, i))]
            sums[b, i] = total
            if plan.mirrored and b:
                upright = jnp.concatenate([total] * T, axis=0).T
                size = SR // T
                for u in range(T):
                    packed = jnp.zeros((size, R), jnp.float32)
                    for k in range(T):
                        lines = upright[u * SR + k * size : u * SR + (k + 1) * size]
                        packed = jnp.where(lane_set == k, lines, packed)
                    turned[b][i, u] = packed
                for w in range(T):
                    u = term_peer(w)
                    begin(
                        remote(
                            turned[b].at[i, u], mirror[b].at[lax.div(m, 2), t], send_m.at[b, i, w],
                            recv_m.at[b, lax.div(m, 2), t],
                            groups[b] * M + column_member(g, groups[b], i), u,
                        )
                    )

    for o in range(1, D):
        p = doc_peer(o)
        remote(sq_doc.at[p], sq_doc.at[p], send_sd.at[o], recv_sd.at[p], p, t).wait_recv()
    pick = lax.broadcasted_iota(jnp.int32, (SR, R), 1) == (
        lax.broadcasted_iota(jnp.int32, (SR, R), 0) + t * SR
    )
    own_column = jnp.sum(jnp.where(pick, sq_doc[d][0:1], 0.0), axis=1, keepdims=True)
    row_norm = jnp.sqrt(own_column + epsilon)

    def finish(total, c):
        norms = row_norm * jnp.sqrt(sq_doc[c][0:1] + epsilon)
        out[:, pl.ds(pl.multiple_of(c * R, R), R)] = total / norms

    for b, i in sums:
        finish(sums[b, i], groups[b] * M + (column_member(g, groups[b], i) if b else i))
    if plan.mirrored:
        for b in range(1, G):
            for i in range(H):
                c = groups[b] * M + mirror_member(b, i)
                for u in range(T):
                    remote(
                        turned[b].at[i, u], mirror[b].at[i, u], send_m.at[b, i, u],
                        recv_m.at[b, i, u], c, t,
                    ).wait_recv()
                lines = []
                for k in range(T):
                    line = jnp.zeros((SR // T, R), jnp.float32)
                    for u in range(T):
                        piece = mirror[b][i, u]
                        if u != k:
                            piece = pltpu.roll(piece, (u - k) % T * SR, 1)
                        line = jnp.where(lane_set == u, piece, line)
                    lines.append(line)
                finish(jnp.concatenate(lines, axis=0), c)

    for copy in pending:
        copy.wait_send()


def shards(doc_tiles, tile_list):
    D = lax.axis_size("doc")
    T = lax.axis_size("term")
    R, N, W = doc_tiles.shape
    plan = Plan(D, T, R, N, W)
    G, M, H, L, SR = plan.G, plan.M, plan.H, plan.L, plan.SR
    many = lambda *shape: pltpu.SemaphoreType.DMA(shape)
    buffer = lambda *shape: pltpu.VMEM(tuple(max(n, 1) for n in shape), jnp.float32)
    scratch = [pltpu.VMEM((M * (N + 1), R, L), doc_tiles.dtype) for _ in range(G)]
    numbers = [len(plan.blocks(*key)) for key in plan.sets()]
    scratch += [buffer(plan.count(a ^ b), R, R) for a, b in plan.direct()]
    scratch += [buffer(plan.count(a ^ b), R, R) for a, b in plan.direct() if a]
    scratch += [buffer(n, R, R) for n in numbers]
    scratch += [buffer(T - 1, n, SR, R) for n in numbers]
    scratch += [buffer(n, SR, R) for n in numbers]
    scratch += [buffer(n, SR, R) for n in numbers]
    scratch += [buffer(plan.count(b), R, R) for b in range(G)]
    scratch += [buffer(T - 1, plan.count(b), SR, R) for b in range(G)]
    if plan.mirrored:
        scratch += [buffer(H, T, SR // T, R) for _ in range(1, G)]
        scratch += [buffer(H, T, SR // T, R) for _ in range(1, G)]
    scratch += [pltpu.VMEM((R * N, L), doc_tiles.dtype) for _ in range(G)]
    scratch += [pltpu.VMEM((N, R, L), doc_tiles.dtype) for _ in range(1, G)]
    scratch += [pltpu.VMEM((plan.rows * N, plan.rows * N), doc_tiles.dtype)]
    scratch += [buffer(T, 8, R), buffer(D, 8, R)]
    scratch += [pltpu.VMEM((G * D, LANES), jnp.int32), pltpu.SMEM((G * D, LANES), jnp.int32)]
    scratch += [
        many(G), pltpu.SemaphoreType.DMA,
        many(G, plan.parts), many(G, M, plan.parts), many(G, M, plan.parts),
        many(T), many(T), many(D), many(D),
        many(G, G), many(G, G), many(G, M, T), many(G, M, T),
        many(G, T), many(G, T), many(2, G, T), many(2, G, T), many(2, G), many(2, G),
    ]
    return pl.pallas_call(
        functools.partial(body, plan),
        out_shape=jax.ShapeDtypeStruct((SR, D * R), jnp.float32),
        in_specs=[
            pl.BlockSpec(memory_space=pltpu.VMEM),
            pl.BlockSpec(memory_space=pl.ANY),
        ],
        out_specs=pl.BlockSpec(memory_space=pltpu.VMEM),
        scratch_shapes=scratch,
        compiler_params=pltpu.CompilerParams(
            collective_id=0, has_side_effects=True, vmem_limit_bytes=56 * 1024 * 1024
        ),
        cost_estimate=pl.CostEstimate(
            flops=2 * G * R * D * R * N * L,
            bytes_accessed=R * N * W * 2 + SR * D * R * 4,
            transcendentals=0,
        ),
    )(tile_list, doc_tiles.reshape(R * N, W))


def solution(mesh):
    placed = (P("doc", None, "term"), P())
    return jax.shard_map(
        shards, mesh=mesh, in_specs=placed, out_specs=P(("doc", "term"), None), check_vma=False
    )
```

```python
import functools

import jax
import jax.numpy as jnp
from jax import lax
from jax.experimental import pallas as pl
from jax.experimental.pallas import tpu as pltpu
from jax.sharding import PartitionSpec as P

epsilon = 1e-06
LANES = 128
MESH = pl.DeviceIdType.MESH


def flip(g, o):
    bit = 1
    while bit <= o:
        if o & bit:
            g = g + bit - 2 * bit * lax.rem(lax.div(g, bit), 2)
        bit *= 2
    return g


class Plan:
    def __init__(self, D, T, R, N, W):
        G = 1
        while D % (2 * G) == 0 and W % (2 * G * LANES) == 0:
            G *= 2
        self.D, self.T, self.R, self.N, self.W, self.G = D, T, R, N, W, G
        self.M = D // G
        self.L = W // G
        self.SR = R // T
        self.mirrored = (
            G > 1 and self.M % 2 == 0 and R == LANES and self.SR % T == 0 and self.SR // T % 8 == 0
        )
        self.H = self.M // 2 if self.mirrored else self.M
        self.parts = 2 if N % 2 == 0 else 1
        self.step = N // self.parts
        self.rows = 16 if R % 16 == 0 else R

    def count(self, o):
        return self.M if o == 0 else self.H

    def wave(self, a, b):
        return max(self.stage(a), self.stage(b))

    def term_first(self, a, b):
        return a > 0 and (self.wave(a, b) == 1 or a == b)

    def blocks(self, wave, a):
        if wave == 0:
            return []
        return [
            (b, i)
            for b in range(self.G)
            if self.wave(a, b) == wave and self.term_first(a, b)
            for i in range(self.count(a ^ b))
        ]

    def sets(self):
        return [(w, a) for w in (1, 2) for a in range(1, self.G) if self.blocks(w, a)]

    def direct(self):
        return [
            (a, b) for a in range(self.G) for b in range(self.G) if not self.term_first(a, b)
        ]

    def stage(self, o):
        return 0 if o == 0 else 1 if o & (o - 1) == 0 else 2


def body(plan, names, docs, out, *scratch):
    D, T, G, M, H = plan.D, plan.T, plan.G, plan.M, plan.H
    R, N, L, SR = plan.R, plan.N, plan.L, plan.SR
    scratch = list(scratch)
    take = lambda n: [scratch.pop(0) for _ in range(n)]
    tiles = take(G)
    part = {pair: take(1)[0] for pair in plan.direct()}
    got = {pair: take(1)[0] for pair in plan.direct() if pair[0]}
    early = {key: take(1)[0] for key in plan.sets()}
    early_z = {key: take(1)[0] for key in plan.sets()}
    early_sum = {key: take(1)[0] for key in plan.sets()}
    early_xy = {key: take(1)[0] for key in plan.sets()}
    whole = {b: take(1)[0] for b in range(G)}
    got_z = {b: take(1)[0] for b in range(G)}
    if plan.mirrored:
        turned = {b: take(1)[0] for b in range(1, G)}
        mirror = {b: take(1)[0] for b in range(1, G)}
    raw = take(G)
    ranges = [None] + take(G - 1)
    order, sq_term, sq_doc, table_rows, table = take(5)
    (
        raw_sem, table_sem, send_a, recv_a, send_f, send_st, recv_st, send_sd, recv_sd,
        send_p, recv_p, send_m, recv_m, send_z, recv_z, send_ez, recv_ez, send_ex, recv_ex,
    ) = scratch

    d = lax.axis_index("doc")
    t = lax.axis_index("term")
    g = lax.div(d, M)
    m = lax.rem(d, M)
    groups = [flip(g, o) for o in range(G)]

    def doc_peer(o):
        return lax.rem(d + o, D)

    def term_peer(o):
        return lax.rem(t + o, T)

    def sibling(i):
        return lax.rem(m + i, M)

    def remote(src, dst, ssem, rsem, doc, term):
        return pltpu.make_async_remote_copy(
            src_ref=src, dst_ref=dst, send_sem=ssem, recv_sem=rsem,
            device_id=(doc, term), device_id_type=MESH,
        )

    def column_member(row_group, column_group, i):
        if not plan.mirrored:
            return i
        return 2 * i + lax.rem(m + jnp.where(row_group < column_group, 1, 0), 2)

    parts, step = plan.parts, plan.step

    def slot(o, member, h):
        return tiles[o].at[pl.ds(member * (N + 1) + h * step, step)]

    def cut(group):
        if G == 1:
            return docs
        return docs.at[:, pl.ds(pl.multiple_of(group * L, L), L)]

    first = [o for o in range(1, G) if plan.stage(o) == 1]
    second = [o for o in range(1, G) if plan.stage(o) == 2]
    loads = {}
    for o in first + [0] + second:
        loads[o] = pltpu.make_async_copy(cut(groups[o]), raw[o], raw_sem.at[o])
        loads[o].start()

    barrier = pltpu.get_barrier_semaphore()
    greeted = [
        (o, u) for o in range(D) for u in range(T) if o + u and (plan.mirrored or not o * u)
    ]
    for o, u in greeted:
        pl.semaphore_signal(
            barrier, inc=1, device_id=(doc_peer(o), term_peer(u)), device_id_type=MESH
        )
    pending = []

    def begin(copy):
        copy.start()
        pending.append(copy)
        return copy

    def send_range(o, h):
        return begin(
            remote(
                ranges[o].at[pl.ds(h * step, step)], slot(o, m, h), send_a.at[o, h],
                recv_a.at[o, m, h], groups[o] * M + m, t,
            )
        )

    def hand_on(o, h):
        for i in range(1, M):
            begin(
                remote(
                    slot(o, m, h), slot(o, m, h), send_f.at[o, i, h], recv_a.at[o, m, h],
                    g * M + sibling(i), t,
                )
            )

    def take_over(o):
        for h in range(parts):
            for i in range(1, M):
                other = sibling(i)
                remote(
                    slot(o, other, h), slot(o, other, h), send_f.at[o, i, h], recv_a.at[o, other, h],
                    g * M + other, t,
                ).wait_recv()

    def arrived(o, h):
        remote(
            slot(o, m, h), slot(o, m, h), send_a.at[o, h], recv_a.at[o, m, h], groups[o] * M + m, t
        ).wait_recv()
        hand_on(o, h)

    def slots_first(o):
        loads[o].wait()

        def some_rows(k, carry):
            rows = pl.ds(pl.multiple_of(k * plan.rows, plan.rows), plan.rows)
            held = raw[o][pl.ds(pl.multiple_of(k * plan.rows * N, plan.rows * N), plan.rows * N), :]
            value = jnp.dot(order[...], held, preferred_element_type=jnp.float32)
            value = value.astype(docs.dtype).reshape(N, plan.rows, L)
            if o:
                ranges[o][:, rows, :] = value
            else:
                tiles[0][pl.ds(m * (N + 1), N), rows, :] = value
            return carry

        lax.fori_loop(0, R // plan.rows, some_rows, 0)

    size = plan.rows * N
    origin = jnp.concatenate(
        [lax.broadcasted_iota(jnp.int32, (plan.rows, 1), 0) * N + a for a in range(N)], axis=0
    )
    hit = origin == lax.broadcasted_iota(jnp.int32, (size, size), 1)
    order[...] = jnp.where(hit, 1.0, 0.0).astype(docs.dtype)

    first_sends = []
    if first:
        slots_first(first[0])
    if greeted:
        pl.semaphore_wait(barrier, len(greeted))
    for o in first:
        if o != first[0]:
            slots_first(o)
        for h in range(parts):
            first_sends.append(send_range(o, h))
    slots_first(0)
    for h in range(parts):
        hand_on(0, h)
    for o in second:
        slots_first(o)
        for h in range(parts - 1):
            send_range(o, h)

    for o in range(G):
        for member in range(M):
            tiles[o][member * (N + 1) + N] = jnp.zeros((R, L), docs.dtype)
    same = lax.broadcasted_iota(jnp.int32, (N, N), 0) == lax.broadcasted_iota(jnp.int32, (N, N), 1)
    place = lax.broadcasted_iota(jnp.int32, (N, N), 0)
    for c in range(D):
        upright = jnp.sum(jnp.where(same, names[c : c + 1, :], 0), axis=1, keepdims=True)
        for a in range(G):
            line = names[pl.ds(groups[a] * M + m, 1), :]
            found = jnp.where(upright == line, place, N)
            table_rows[a * D + c : a * D + c + 1, 0:N] = jnp.min(found, axis=0, keepdims=True)
    to_scalars = pltpu.make_async_copy(table_rows, table, table_sem)
    to_scalars.start()

    def add_square(a, total):
        for q in range(G):
            held = ranges[q][a] if q else tiles[0][m * (N + 1) + a]
            value = held.astype(jnp.float32)
            total = total + value * value
        return total

    square = lax.fori_loop(0, N, add_square, jnp.zeros((R, L), jnp.float32))
    column = jnp.sum(square, axis=1, keepdims=True)
    eye = lax.broadcasted_iota(jnp.int32, (R, R), 0) == lax.broadcasted_iota(jnp.int32, (R, R), 1)
    row = jnp.sum(jnp.where(eye, column, 0.0), axis=0, keepdims=True)
    sq_term[t] = jnp.broadcast_to(row, (8, R))
    for o in range(1, T):
        begin(remote(sq_term.at[t], sq_term.at[t], send_st.at[o], recv_st.at[t], d, term_peer(o)))
    for o in range(1, T):
        p = term_peer(o)
        remote(sq_term.at[p], sq_term.at[p], send_st.at[o], recv_st.at[p], d, p).wait_recv()
    total = sq_term[0]
    for q in range(1, T):
        total = total + sq_term[q]
    sq_doc[d] = total
    for o in range(1, D):
        begin(remote(sq_doc.at[d], sq_doc.at[d], send_sd.at[o], recv_sd.at[d], doc_peer(o), t))

    def over_term(source, landing, ssem, rsem):
        for o in range(1, T):
            p = term_peer(o)
            begin(
                remote(
                    source.at[:, pl.ds(p * SR, SR), :], landing.at[o - 1], ssem.at[o], rsem.at[o], d, p
                )
            )

    def products(a, wanted_blocks):
        own = jnp.concatenate([tiles[a][m * (N + 1) + e] for e in range(N)], axis=1)
        others = []
        for b, i, target, place in wanted_blocks:
            member = i if a == b else column_member(groups[a], groups[b], i)
            line = a * D + groups[b] * M + member
            others.append(
                jnp.concatenate(
                    [tiles[b][member * (N + 1) + table[line, e]] for e in range(N)], axis=1
                )
            )
        result = lax.dot_general(
            jnp.concatenate(others, axis=0), own, (((1,), (1,)), ((), ())),
            preferred_element_type=jnp.float32,
        )
        for k, (b, i, target, place) in enumerate(wanted_blocks):
            target[place] = result[k * R : (k + 1) * R].T

    def rows_of(wave, a):
        columns = [b for b in range(G) if plan.wave(a, b) == wave]
        if not columns:
            return
        jobs = []
        for b in columns:
            if plan.term_first(a, b):
                target, base = early[wave, a], plan.blocks(wave, a).index((b, 0))
            else:
                target, base = part[a, b], 0
            jobs.append((b, target, base))
        if sum(plan.count(a ^ b) for b in columns) <= 8:
            products(
                a, [(b, i, x, base + i) for b, x, base in jobs for i in range(plan.count(a ^ b))]
            )
        else:
            for b, x, base in jobs:
                def one(i, carry, b=b, x=x, base=base):
                    products(a, [(b, i, x, base + i)])
                    return carry

                lax.fori_loop(0, plan.count(a ^ b), one, 0)
        if plan.blocks(wave, a):
            over_term(
                early[wave, a], early_z[wave, a], send_ez.at[wave - 1, a], recv_ez.at[wave - 1, a]
            )
        for b in columns:
            if a and not plan.term_first(a, b):
                begin(
                    remote(
                        part[a, b], got[a, b], send_p.at[a, b], recv_p.at[a, b],
                        groups[a] * M + m, t,
                    )
                )

    wanted = list(range(1, G)) + [0]

    def pairs(wave):
        for a in sorted(range(G), key=lambda a: (a == 0, -plan.stage(a))):
            rows_of(wave, a)

    to_scalars.wait()
    take_over(0)
    pairs(0)
    for h in range(parts):
        for o in first:
            arrived(o, h)
    for copy in first_sends:
        copy.wait_send()
        pending.remove(copy)
    for o in second:
        send_range(o, parts - 1)
    for o in first:
        take_over(o)
    if first:
        pairs(1)
    for h in range(parts):
        for o in second:
            arrived(o, h)
    for o in second:
        take_over(o)
    if second:
        pairs(2)

    def pass_early(wave):
        for w, a in [key for key in plan.sets() if key[0] == wave]:
            for o in range(1, T):
                remote(
                    early[w, a].at[:, pl.ds(t * SR, SR), :], early_z[w, a].at[o - 1],
                    send_ez.at[w - 1, a, o], recv_ez.at[w - 1, a, o], d, term_peer(o),
                ).wait_recv()
            for i in range(len(plan.blocks(w, a))):
                total = early[w, a][i, pl.ds(pl.multiple_of(t * SR, SR), SR), :]
                for o in range(1, T):
                    total = total + early_z[w, a][o - 1, i]
                early_sum[w, a][i] = total
            begin(
                remote(
                    early_sum[w, a], early_xy[w, a], send_ex.at[w - 1, a], recv_ex.at[w - 1, a],
                    groups[a] * M + m, t,
                )
            )

    pass_early(1)
    for b in wanted:
        direct = [a for a in range(1, G) if not plan.term_first(a, a ^ b)]
        for a in direct:
            remote(
                part[a, a ^ b], got[a, a ^ b], send_p.at[a, a ^ b], recv_p.at[a, a ^ b],
                groups[a] * M + m, t,
            ).wait_recv()
        for i in range(plan.count(b)):
            total = part[0, b][i]
            for a in direct:
                total = total + got[a, a ^ b][i]
            whole[b][i] = total
        over_term(whole[b], got_z[b], send_z.at[b], recv_z.at[b])
    pass_early(2)

    def mirror_member(b, i):
        return 2 * i + lax.rem(m + jnp.where(groups[b] < g, 1, 0), 2)

    lane_set = lax.div(lax.broadcasted_iota(jnp.int32, (max(SR // T, 1), R), 1), SR)
    for w, a in plan.sets():
        remote(
            early_sum[w, a], early_xy[w, a], send_ex.at[w - 1, a], recv_ex.at[w - 1, a],
            groups[a] * M + m, t,
        ).wait_recv()
    sums = {}
    for b in wanted:
        for o in range(1, T):
            remote(
                whole[b].at[:, pl.ds(t * SR, SR), :], got_z[b].at[o - 1], send_z.at[b, o],
                recv_z.at[b, o], d, term_peer(o),
            ).wait_recv()
        for i in range(plan.count(b)):
            total = whole[b][i, pl.ds(pl.multiple_of(t * SR, SR), SR), :]
            for o in range(1, T):
                total = total + got_z[b][o - 1, i]
            for a in range(1, G):
                if plan.term_first(a, a ^ b):
                    wave = plan.wave(a, a ^ b)
                    total = total + early_xy[wave, a][plan.blocks(wave, a).index((a ^ b, i))]
            sums[b, i] = total
            if plan.mirrored and b:
                upright = jnp.concatenate([total] * T, axis=0).T
                size = SR // T
                for u in range(T):
                    packed = jnp.zeros((size, R), jnp.float32)
                    for k in range(T):
                        lines = upright[u * SR + k * size : u * SR + (k + 1) * size]
                        packed = jnp.where(lane_set == k, lines, packed)
                    turned[b][i, u] = packed
                for w in range(T):
                    u = term_peer(w)
                    begin(
                        remote(
                            turned[b].at[i, u], mirror[b].at[lax.div(m, 2), t], send_m.at[b, i, w],
                            recv_m.at[b, lax.div(m, 2), t],
                            groups[b] * M + column_member(g, groups[b], i), u,
                        )
                    )

    for o in range(1, D):
        p = doc_peer(o)
        remote(sq_doc.at[p], sq_doc.at[p], send_sd.at[o], recv_sd.at[p], p, t).wait_recv()
    pick = lax.broadcasted_iota(jnp.int32, (SR, R), 1) == (
        lax.broadcasted_iota(jnp.int32, (SR, R), 0) + t * SR
    )
    own_column = jnp.sum(jnp.where(pick, sq_doc[d][0:1], 0.0), axis=1, keepdims=True)
    row_norm = jnp.sqrt(own_column + epsilon)

    def finish(total, c):
        norms = row_norm * jnp.sqrt(sq_doc[c][0:1] + epsilon)
        out[:, pl.ds(pl.multiple_of(c * R, R), R)] = total / norms

    for b, i in sums:
        finish(sums[b, i], groups[b] * M + (column_member(g, groups[b], i) if b else i))
    if plan.mirrored:
        for b in range(1, G):
            for i in range(H):
                c = groups[b] * M + mirror_member(b, i)
                for u in range(T):
                    remote(
                        turned[b].at[i, u], mirror[b].at[i, u], send_m.at[b, i, u],
                        recv_m.at[b, i, u], c, t,
                    ).wait_recv()
                lines = []
                for k in range(T):
                    line = jnp.zeros((SR // T, R), jnp.float32)
                    for u in range(T):
                        piece = mirror[b][i, u]
                        if u != k:
                            piece = pltpu.roll(piece, (u - k) % T * SR, 1)
                        line = jnp.where(lane_set == u, piece, line)
                    lines.append(line)
                finish(jnp.concatenate(lines, axis=0), c)

    for copy in pending:
        copy.wait_send()


def shards(doc_tiles, tile_list):
    D = lax.axis_size("doc")
    T = lax.axis_size("term")
    R, N, W = doc_tiles.shape
    plan = Plan(D, T, R, N, W)
    G, M, H, L, SR = plan.G, plan.M, plan.H, plan.L, plan.SR
    many = lambda *shape: pltpu.SemaphoreType.DMA(shape)
    buffer = lambda *shape: pltpu.VMEM(tuple(max(n, 1) for n in shape), jnp.float32)
    scratch = [pltpu.VMEM((M * (N + 1), R, L), doc_tiles.dtype) for _ in range(G)]
    numbers = [len(plan.blocks(*key)) for key in plan.sets()]
    scratch += [buffer(plan.count(a ^ b), R, R) for a, b in plan.direct()]
    scratch += [buffer(plan.count(a ^ b), R, R) for a, b in plan.direct() if a]
    scratch += [buffer(n, R, R) for n in numbers]
    scratch += [buffer(T - 1, n, SR, R) for n in numbers]
    scratch += [buffer(n, SR, R) for n in numbers]
    scratch += [buffer(n, SR, R) for n in numbers]
    scratch += [buffer(plan.count(b), R, R) for b in range(G)]
    scratch += [buffer(T - 1, plan.count(b), SR, R) for b in range(G)]
    if plan.mirrored:
        scratch += [buffer(H, T, SR // T, R) for _ in range(1, G)]
        scratch += [buffer(H, T, SR // T, R) for _ in range(1, G)]
    scratch += [pltpu.VMEM((R * N, L), doc_tiles.dtype) for _ in range(G)]
    scratch += [pltpu.VMEM((N, R, L), doc_tiles.dtype) for _ in range(1, G)]
    scratch += [pltpu.VMEM((plan.rows * N, plan.rows * N), doc_tiles.dtype)]
    scratch += [buffer(T, 8, R), buffer(D, 8, R)]
    scratch += [pltpu.VMEM((G * D, LANES), jnp.int32), pltpu.SMEM((G * D, LANES), jnp.int32)]
    scratch += [
        many(G), pltpu.SemaphoreType.DMA,
        many(G, plan.parts), many(G, M, plan.parts), many(G, M, plan.parts),
        many(T), many(T), many(D), many(D),
        many(G, G), many(G, G), many(G, M, T), many(G, M, T),
        many(G, T), many(G, T), many(2, G, T), many(2, G, T), many(2, G), many(2, G),
    ]
    return pl.pallas_call(
        functools.partial(body, plan),
        out_shape=jax.ShapeDtypeStruct((SR, D * R), jnp.float32),
        in_specs=[
            pl.BlockSpec(memory_space=pltpu.VMEM),
            pl.BlockSpec(memory_space=pl.ANY),
        ],
        out_specs=pl.BlockSpec(memory_space=pltpu.VMEM),
        scratch_shapes=scratch,
        compiler_params=pltpu.CompilerParams(
            collective_id=0, has_side_effects=True, vmem_limit_bytes=56 * 1024 * 1024
        ),
        cost_estimate=pl.CostEstimate(
            flops=2 * G * R * D * R * N * L,
            bytes_accessed=R * N * W * 2 + SR * D * R * 4,
            transcendentals=0,
        ),
    )(tile_list, doc_tiles.reshape(R * N, W))


def solution(mesh):
    placed = (P("doc", None, "term"), P())
    return jax.shard_map(
        shards, mesh=mesh, in_specs=placed, out_specs=P(("doc", "term"), None), check_vma=False
    )
```

```python
import functools

import jax
import jax.numpy as jnp
from jax import lax
from jax.experimental import pallas as pl
from jax.experimental.pallas import tpu as pltpu
from jax.sharding import PartitionSpec as P

epsilon = 1e-06
LANES = 128
MESH = pl.DeviceIdType.MESH


def flip(g, o):
    bit = 1
    while bit <= o:
        if o & bit:
            g = g + bit - 2 * bit * lax.rem(lax.div(g, bit), 2)
        bit *= 2
    return g


class Plan:
    def __init__(self, D, T, R, N, W):
        G = 1
        while D % (2 * G) == 0 and W % (2 * G * LANES) == 0:
            G *= 2
        self.D, self.T, self.R, self.N, self.W, self.G = D, T, R, N, W, G
        self.M = D // G
        self.L = W // G
        self.SR = R // T
        self.mirrored = (
            G > 1 and self.M % 2 == 0 and R == LANES and self.SR % T == 0 and self.SR // T % 8 == 0
        )
        self.H = self.M // 2 if self.mirrored else self.M
        self.parts = 2 if R % 32 == 0 else 1
        self.step = R // self.parts
        self.rows = 16 if R % 16 == 0 else R

    def count(self, o):
        return self.M if o == 0 else self.H

    def wave(self, a, b):
        return max(self.stage(a), self.stage(b))

    def term_first(self, a, b):
        return a > 0 and (self.wave(a, b) == 1 or a == b)

    def blocks(self, wave, a):
        return [
            (b, i)
            for b in range(self.G)
            if self.wave(a, b) == wave and self.term_first(a, b)
            for i in range(self.count(a ^ b))
        ]

    def sets(self):
        return [(w, a) for w in (1, 2) for a in range(1, self.G) if self.blocks(w, a)]

    def direct(self):
        return [
            (a, b) for a in range(self.G) for b in range(self.G) if not self.term_first(a, b)
        ]

    def stage(self, o):
        return 0 if o == 0 else 1 if o & (o - 1) == 0 else 2


def body(plan, names, docs, out, *scratch):
    D, T, G, M, H = plan.D, plan.T, plan.G, plan.M, plan.H
    R, N, L, SR = plan.R, plan.N, plan.L, plan.SR
    scratch = list(scratch)
    take = lambda n: [scratch.pop(0) for _ in range(n)]
    tiles = take(G)
    part = {pair: take(1)[0] for pair in plan.direct()}
    got = {pair: take(1)[0] for pair in plan.direct() if pair[0]}
    early = {key: take(1)[0] for key in plan.sets()}
    early_z = {key: take(1)[0] for key in plan.sets()}
    early_sum = {key: take(1)[0] for key in plan.sets()}
    early_xy = {key: take(1)[0] for key in plan.sets()}
    whole = {b: take(1)[0] for b in range(G)}
    got_z = {b: take(1)[0] for b in range(G)}
    if plan.mirrored:
        turned = {b: take(1)[0] for b in range(1, G)}
        mirror = {b: take(1)[0] for b in range(1, G)}
    raw = take(G)
    ranges = [None] + take(G - 1)
    order, sq_term, sq_doc, table_rows, table = take(5)
    (
        raw_sem, table_sem, send_a, recv_a, send_f, send_st, recv_st, send_sd, recv_sd,
        send_p, recv_p, send_m, recv_m, send_z, recv_z, send_ez, recv_ez, send_ex, recv_ex,
    ) = scratch

    d = lax.axis_index("doc")
    t = lax.axis_index("term")
    g = lax.div(d, M)
    m = lax.rem(d, M)
    groups = [flip(g, o) for o in range(G)]

    def doc_peer(o):
        return lax.rem(d + o, D)

    def term_peer(o):
        return lax.rem(t + o, T)

    def sibling(i):
        return lax.rem(m + i, M)

    def remote(src, dst, ssem, rsem, doc, term):
        return pltpu.make_async_remote_copy(
            src_ref=src, dst_ref=dst, send_sem=ssem, recv_sem=rsem,
            device_id=(doc, term), device_id_type=MESH,
        )

    def column_member(row_group, column_group, i):
        if not plan.mirrored:
            return i
        return 2 * i + lax.rem(m + jnp.where(row_group < column_group, 1, 0), 2)

    parts, step = plan.parts, plan.step

    def slot(o, member, h):
        return tiles[o].at[pl.ds(member * (N + 1), N), pl.ds(h * step, step), :]

    def cut(group):
        if G == 1:
            return docs
        return docs.at[:, pl.ds(pl.multiple_of(group * L, L), L)]

    first = [o for o in range(1, G) if plan.stage(o) == 1]
    second = [o for o in range(1, G) if plan.stage(o) == 2]
    loads = {}
    for o in first + [0] + second:
        loads[o] = pltpu.make_async_copy(cut(groups[o]), raw[o], raw_sem.at[o])
        loads[o].start()

    barrier = pltpu.get_barrier_semaphore()
    greeted = [
        (o, u) for o in range(D) for u in range(T) if o + u and (plan.mirrored or not o * u)
    ]
    for o, u in greeted:
        pl.semaphore_signal(
            barrier, inc=1, device_id=(doc_peer(o), term_peer(u)), device_id_type=MESH
        )
    pending = []

    def begin(copy):
        copy.start()
        pending.append(copy)
        return copy

    def send_range(o, h):
        return begin(
            remote(
                ranges[o].at[:, pl.ds(h * step, step), :], slot(o, m, h), send_a.at[o, h],
                recv_a.at[o, m, h], groups[o] * M + m, t,
            )
        )

    def hand_on(o, h):
        for i in range(1, M):
            begin(
                remote(
                    slot(o, m, h), slot(o, m, h), send_f.at[o, i, h], recv_a.at[o, m, h],
                    g * M + sibling(i), t,
                )
            )

    def take_over(o):
        for h in range(parts):
            for i in range(1, M):
                other = sibling(i)
                remote(
                    slot(o, other, h), slot(o, other, h), send_f.at[o, i, h], recv_a.at[o, other, h],
                    g * M + other, t,
                ).wait_recv()

    def arrived(o, h):
        remote(
            slot(o, m, h), slot(o, m, h), send_a.at[o, h], recv_a.at[o, m, h], groups[o] * M + m, t
        ).wait_recv()
        hand_on(o, h)

    def slots_first(o, h):
        if h == 0:
            loads[o].wait()
        few = step // plan.rows

        def some_rows(k, carry):
            rows = pl.ds(pl.multiple_of(k * plan.rows, plan.rows), plan.rows)
            held = raw[o][pl.ds(pl.multiple_of(k * plan.rows * N, plan.rows * N), plan.rows * N), :]
            value = jnp.dot(order[...], held, preferred_element_type=jnp.float32)
            value = value.astype(docs.dtype).reshape(N, plan.rows, L)
            if o:
                ranges[o][:, rows, :] = value
            else:
                tiles[0][pl.ds(m * (N + 1), N), rows, :] = value
            return carry

        lax.fori_loop(h * few, (h + 1) * few, some_rows, 0)

    size = plan.rows * N
    origin = jnp.concatenate(
        [lax.broadcasted_iota(jnp.int32, (plan.rows, 1), 0) * N + a for a in range(N)], axis=0
    )
    hit = origin == lax.broadcasted_iota(jnp.int32, (size, size), 1)
    order[...] = jnp.where(hit, 1.0, 0.0).astype(docs.dtype)

    first_sends = []
    if first:
        slots_first(first[0], 0)
    if greeted:
        pl.semaphore_wait(barrier, len(greeted))
    for h in range(parts):
        for o in first:
            if (o, h) != (first[0], 0):
                slots_first(o, h)
            first_sends.append(send_range(o, h))
    for h in range(parts):
        slots_first(0, h)
        hand_on(0, h)
    for o in second:
        for h in range(parts):
            slots_first(o, h)
            if h < parts - 1:
                send_range(o, h)

    for o in range(G):
        tiles[o][m * (N + 1) + N] = jnp.zeros((R, L), docs.dtype)
    same = lax.broadcasted_iota(jnp.int32, (N, N), 0) == lax.broadcasted_iota(jnp.int32, (N, N), 1)
    place = lax.broadcasted_iota(jnp.int32, (N, N), 0)
    for a in range(G):
        line = names[pl.ds(groups[a] * M + m, 1), :]
        upright = jnp.sum(jnp.where(same, line, 0), axis=1, keepdims=True)
        for c in range(D):
            found = jnp.where(upright == names[c : c + 1, :], place, N)
            table_rows[a * D + c : a * D + c + 1, 0:N] = jnp.min(found, axis=0, keepdims=True)
    to_scalars = pltpu.make_async_copy(table_rows, table, table_sem)
    to_scalars.start()

    def add_square(a, total):
        for q in range(G):
            held = ranges[q][a] if q else tiles[0][m * (N + 1) + a]
            value = held.astype(jnp.float32)
            total = total + value * value
        return total

    square = lax.fori_loop(0, N, add_square, jnp.zeros((R, L), jnp.float32))
    column = jnp.sum(square, axis=1, keepdims=True)
    eye = lax.broadcasted_iota(jnp.int32, (R, R), 0) == lax.broadcasted_iota(jnp.int32, (R, R), 1)
    row = jnp.sum(jnp.where(eye, column, 0.0), axis=0, keepdims=True)
    sq_term[t] = jnp.broadcast_to(row, (8, R))
    for o in range(1, T):
        begin(remote(sq_term.at[t], sq_term.at[t], send_st.at[o], recv_st.at[t], d, term_peer(o)))
    for o in range(1, T):
        p = term_peer(o)
        remote(sq_term.at[p], sq_term.at[p], send_st.at[o], recv_st.at[p], d, p).wait_recv()
    total = sq_term[0]
    for q in range(1, T):
        total = total + sq_term[q]
    sq_doc[d] = total
    for o in range(1, D):
        begin(remote(sq_doc.at[d], sq_doc.at[d], send_sd.at[o], recv_sd.at[d], doc_peer(o), t))

    def over_term(source, landing, ssem, rsem):
        for o in range(1, T):
            p = term_peer(o)
            begin(
                remote(
                    source.at[:, pl.ds(p * SR, SR), :], landing.at[o - 1], ssem.at[o], rsem.at[o], d, p
                )
            )

    def pair(a, b):
        wave = plan.wave(a, b)
        if plan.term_first(a, b):
            target, base = early[wave, a], plan.blocks(wave, a).index((b, 0))
        else:
            target, base = part[a, b], 0

        def one(i, carry):
            member = i if a == b else column_member(groups[a], groups[b], i)
            line = a * D + groups[b] * M + member
            left = jnp.concatenate(
                [tiles[a][m * (N + 1) + table[line, e]] for e in range(N)], axis=1
            )
            right = jnp.concatenate([tiles[b][member * (N + 1) + e] for e in range(N)], axis=1)
            target[base + i] = lax.dot_general(
                left, right, (((1,), (1,)), ((), ())), preferred_element_type=jnp.float32
            )
            return carry

        number = plan.count(a ^ b)
        if number == 1:
            one(0, 0)
        else:
            lax.fori_loop(0, number, one, 0)
        if plan.term_first(a, b):
            if plan.blocks(wave, a)[-1][0] == b:
                over_term(
                    early[wave, a], early_z[wave, a], send_ez.at[wave - 1, a], recv_ez.at[wave - 1, a]
                )
        elif a:
            begin(
                remote(
                    part[a, b], got[a, b], send_p.at[a, b], recv_p.at[a, b], groups[a] * M + m, t
                )
            )

    wanted = list(range(1, G)) + [0]

    def pairs(stage):
        todo = [
            (a, b)
            for a in range(G)
            for b in range(G)
            if plan.wave(a, b) == stage
        ]
        for a, b in [p for p in todo if plan.term_first(*p)]:
            pair(a, b)
        rest = [p for p in todo if not plan.term_first(*p)]
        for a, b in sorted(rest, key=lambda ab: (wanted.index(ab[0] ^ ab[1]), -ab[0])):
            pair(a, b)

    to_scalars.wait()
    take_over(0)
    pairs(0)
    for h in range(parts):
        for o in first:
            arrived(o, h)
    for copy in first_sends:
        copy.wait_send()
        pending.remove(copy)
    for o in second:
        send_range(o, parts - 1)
    for o in first:
        take_over(o)
    if first:
        pairs(1)
    for h in range(parts):
        for o in second:
            arrived(o, h)
    for o in second:
        take_over(o)
    if second:
        pairs(2)

    def pass_early(wave):
        for w, a in [key for key in plan.sets() if key[0] == wave]:
            for o in range(1, T):
                remote(
                    early[w, a].at[:, pl.ds(t * SR, SR), :], early_z[w, a].at[o - 1],
                    send_ez.at[w - 1, a, o], recv_ez.at[w - 1, a, o], d, term_peer(o),
                ).wait_recv()
            for i in range(len(plan.blocks(w, a))):
                total = early[w, a][i, pl.ds(pl.multiple_of(t * SR, SR), SR), :]
                for o in range(1, T):
                    total = total + early_z[w, a][o - 1, i]
                early_sum[w, a][i] = total
            begin(
                remote(
                    early_sum[w, a], early_xy[w, a], send_ex.at[w - 1, a], recv_ex.at[w - 1, a],
                    groups[a] * M + m, t,
                )
            )

    pass_early(1)
    for b in wanted:
        direct = [a for a in range(1, G) if not plan.term_first(a, a ^ b)]
        for a in direct:
            remote(
                part[a, a ^ b], got[a, a ^ b], send_p.at[a, a ^ b], recv_p.at[a, a ^ b],
                groups[a] * M + m, t,
            ).wait_recv()
        for i in range(plan.count(b)):
            total = part[0, b][i]
            for a in direct:
                total = total + got[a, a ^ b][i]
            whole[b][i] = total
        over_term(whole[b], got_z[b], send_z.at[b], recv_z.at[b])
    pass_early(2)

    def mirror_member(b, i):
        return 2 * i + lax.rem(m + jnp.where(groups[b] < g, 1, 0), 2)

    lane_set = lax.div(lax.broadcasted_iota(jnp.int32, (max(SR // T, 1), R), 1), SR)
    for w, a in plan.sets():
        remote(
            early_sum[w, a], early_xy[w, a], send_ex.at[w - 1, a], recv_ex.at[w - 1, a],
            groups[a] * M + m, t,
        ).wait_recv()
    sums = {}
    for b in wanted:
        for o in range(1, T):
            remote(
                whole[b].at[:, pl.ds(t * SR, SR), :], got_z[b].at[o - 1], send_z.at[b, o],
                recv_z.at[b, o], d, term_peer(o),
            ).wait_recv()
        for i in range(plan.count(b)):
            total = whole[b][i, pl.ds(pl.multiple_of(t * SR, SR), SR), :]
            for o in range(1, T):
                total = total + got_z[b][o - 1, i]
            for a in range(1, G):
                if plan.term_first(a, a ^ b):
                    wave = plan.wave(a, a ^ b)
                    total = total + early_xy[wave, a][plan.blocks(wave, a).index((a ^ b, i))]
            sums[b, i] = total
            if plan.mirrored and b:
                upright = jnp.concatenate([total] * T, axis=0).T
                size = SR // T
                for u in range(T):
                    packed = jnp.zeros((size, R), jnp.float32)
                    for k in range(T):
                        lines = upright[u * SR + k * size : u * SR + (k + 1) * size]
                        packed = jnp.where(lane_set == k, lines, packed)
                    turned[b][i, u] = packed
                for w in range(T):
                    u = term_peer(w)
                    begin(
                        remote(
                            turned[b].at[i, u], mirror[b].at[lax.div(m, 2), t], send_m.at[b, i, w],
                            recv_m.at[b, lax.div(m, 2), t],
                            groups[b] * M + column_member(g, groups[b], i), u,
                        )
                    )

    for o in range(1, D):
        p = doc_peer(o)
        remote(sq_doc.at[p], sq_doc.at[p], send_sd.at[o], recv_sd.at[p], p, t).wait_recv()
    pick = lax.broadcasted_iota(jnp.int32, (SR, R), 1) == (
        lax.broadcasted_iota(jnp.int32, (SR, R), 0) + t * SR
    )
    own_column = jnp.sum(jnp.where(pick, sq_doc[d][0:1], 0.0), axis=1, keepdims=True)
    row_norm = jnp.sqrt(own_column + epsilon)

    def finish(total, c):
        norms = row_norm * jnp.sqrt(sq_doc[c][0:1] + epsilon)
        out[:, pl.ds(pl.multiple_of(c * R, R), R)] = total / norms

    for b, i in sums:
        finish(sums[b, i], groups[b] * M + (column_member(g, groups[b], i) if b else i))
    if plan.mirrored:
        for b in range(1, G):
            for i in range(H):
                c = groups[b] * M + mirror_member(b, i)
                for u in range(T):
                    remote(
                        turned[b].at[i, u], mirror[b].at[i, u], send_m.at[b, i, u],
                        recv_m.at[b, i, u], c, t,
                    ).wait_recv()
                lines = []
                for k in range(T):
                    line = jnp.zeros((SR // T, R), jnp.float32)
                    for u in range(T):
                        piece = mirror[b][i, u]
                        if u != k:
                            piece = pltpu.roll(piece, (u - k) % T * SR, 1)
                        line = jnp.where(lane_set == u, piece, line)
                    lines.append(line)
                finish(jnp.concatenate(lines, axis=0), c)

    for copy in pending:
        copy.wait_send()


def shards(doc_tiles, tile_list):
    D = lax.axis_size("doc")
    T = lax.axis_size("term")
    R, N, W = doc_tiles.shape
    plan = Plan(D, T, R, N, W)
    G, M, H, L, SR = plan.G, plan.M, plan.H, plan.L, plan.SR
    many = lambda *shape: pltpu.SemaphoreType.DMA(shape)
    buffer = lambda *shape: pltpu.VMEM(tuple(max(n, 1) for n in shape), jnp.float32)
    scratch = [pltpu.VMEM((M * (N + 1), R, L), doc_tiles.dtype) for _ in range(G)]
    numbers = [len(plan.blocks(*key)) for key in plan.sets()]
    scratch += [buffer(plan.count(a ^ b), R, R) for a, b in plan.direct()]
    scratch += [buffer(plan.count(a ^ b), R, R) for a, b in plan.direct() if a]
    scratch += [buffer(n, R, R) for n in numbers]
    scratch += [buffer(T - 1, n, SR, R) for n in numbers]
    scratch += [buffer(n, SR, R) for n in numbers]
    scratch += [buffer(n, SR, R) for n in numbers]
    scratch += [buffer(plan.count(b), R, R) for b in range(G)]
    scratch += [buffer(T - 1, plan.count(b), SR, R) for b in range(G)]
    if plan.mirrored:
        scratch += [buffer(H, T, SR // T, R) for _ in range(1, G)]
        scratch += [buffer(H, T, SR // T, R) for _ in range(1, G)]
    scratch += [pltpu.VMEM((R * N, L), doc_tiles.dtype) for _ in range(G)]
    scratch += [pltpu.VMEM((N, R, L), doc_tiles.dtype) for _ in range(1, G)]
    scratch += [pltpu.VMEM((plan.rows * N, plan.rows * N), doc_tiles.dtype)]
    scratch += [buffer(T, 8, R), buffer(D, 8, R)]
    scratch += [pltpu.VMEM((G * D, LANES), jnp.int32), pltpu.SMEM((G * D, LANES), jnp.int32)]
    scratch += [
        many(G), pltpu.SemaphoreType.DMA,
        many(G, plan.parts), many(G, M, plan.parts), many(G, M, plan.parts),
        many(T), many(T), many(D), many(D),
        many(G, G), many(G, G), many(G, M, T), many(G, M, T),
        many(G, T), many(G, T), many(2, G, T), many(2, G, T), many(2, G), many(2, G),
    ]
    return pl.pallas_call(
        functools.partial(body, plan),
        out_shape=jax.ShapeDtypeStruct((SR, D * R), jnp.float32),
        in_specs=[
            pl.BlockSpec(memory_space=pltpu.VMEM),
            pl.BlockSpec(memory_space=pl.ANY),
        ],
        out_specs=pl.BlockSpec(memory_space=pltpu.VMEM),
        scratch_shapes=scratch,
        compiler_params=pltpu.CompilerParams(
            collective_id=0, has_side_effects=True, vmem_limit_bytes=56 * 1024 * 1024
        ),
        cost_estimate=pl.CostEstimate(
            flops=2 * G * R * D * R * N * L,
            bytes_accessed=R * N * W * 2 + SR * D * R * 4,
            transcendentals=0,
        ),
    )(tile_list, doc_tiles.reshape(R * N, W))


def solution(mesh):
    placed = (P("doc", None, "term"), P())
    return jax.shard_map(
        shards, mesh=mesh, in_specs=placed, out_specs=P(("doc", "term"), None), check_vma=False
    )
```

```python
import functools

import jax
import jax.numpy as jnp
from jax import lax
from jax.experimental import pallas as pl
from jax.experimental.pallas import tpu as pltpu
from jax.sharding import PartitionSpec as P

epsilon = 1e-06
LANES = 128
MESH = pl.DeviceIdType.MESH


def flip(g, o):
    bit = 1
    while bit <= o:
        if o & bit:
            g = g + bit - 2 * bit * lax.rem(lax.div(g, bit), 2)
        bit *= 2
    return g


class Plan:
    def __init__(self, D, T, R, N, W):
        G = 1
        while D % (2 * G) == 0 and W % (2 * G * LANES) == 0:
            G *= 2
        self.D, self.T, self.R, self.N, self.W, self.G = D, T, R, N, W, G
        self.M = D // G
        self.L = W // G
        self.SR = R // T
        self.mirrored = (
            G > 1 and self.M % 2 == 0 and R == LANES and self.SR % T == 0 and self.SR // T % 8 == 0
        )
        self.H = self.M // 2 if self.mirrored else self.M
        self.parts = 1
        self.step = N // self.parts
        self.rows = 16 if R % 16 == 0 else R

    def count(self, o):
        return self.M if o == 0 else self.H

    def wave(self, a, b):
        return max(self.stage(a), self.stage(b))

    def term_first(self, a, b):
        return a > 0 and (self.wave(a, b) == 1 or a == b)

    def blocks(self, wave, a):
        return [
            (b, i)
            for b in range(self.G)
            if self.wave(a, b) == wave and self.term_first(a, b)
            for i in range(self.count(a ^ b))
        ]

    def sets(self):
        return [(w, a) for w in (1, 2) for a in range(1, self.G) if self.blocks(w, a)]

    def direct(self):
        return [
            (a, b) for a in range(self.G) for b in range(self.G) if not self.term_first(a, b)
        ]

    def stage(self, o):
        return 0 if o == 0 else 1 if o & (o - 1) == 0 else 2


def body(plan, names, docs, out, *scratch):
    D, T, G, M, H = plan.D, plan.T, plan.G, plan.M, plan.H
    R, N, L, SR = plan.R, plan.N, plan.L, plan.SR
    scratch = list(scratch)
    take = lambda n: [scratch.pop(0) for _ in range(n)]
    tiles = take(G)
    part = {pair: take(1)[0] for pair in plan.direct()}
    got = {pair: take(1)[0] for pair in plan.direct() if pair[0]}
    early = {key: take(1)[0] for key in plan.sets()}
    early_z = {key: take(1)[0] for key in plan.sets()}
    early_sum = {key: take(1)[0] for key in plan.sets()}
    early_xy = {key: take(1)[0] for key in plan.sets()}
    whole = {b: take(1)[0] for b in range(G)}
    got_z = {b: take(1)[0] for b in range(G)}
    if plan.mirrored:
        turned = {b: take(1)[0] for b in range(1, G)}
        mirror = {b: take(1)[0] for b in range(1, G)}
    raw = take(G)
    ranges = [None] + take(G - 1)
    order, sq_term, sq_doc, table_rows, table = take(5)
    (
        raw_sem, table_sem, send_a, recv_a, send_f, send_st, recv_st, send_sd, recv_sd,
        send_p, recv_p, send_m, recv_m, send_z, recv_z, send_ez, recv_ez, send_ex, recv_ex,
    ) = scratch

    d = lax.axis_index("doc")
    t = lax.axis_index("term")
    g = lax.div(d, M)
    m = lax.rem(d, M)
    groups = [flip(g, o) for o in range(G)]

    def doc_peer(o):
        return lax.rem(d + o, D)

    def term_peer(o):
        return lax.rem(t + o, T)

    def sibling(i):
        return lax.rem(m + i, M)

    def remote(src, dst, ssem, rsem, doc, term):
        return pltpu.make_async_remote_copy(
            src_ref=src, dst_ref=dst, send_sem=ssem, recv_sem=rsem,
            device_id=(doc, term), device_id_type=MESH,
        )

    def column_member(row_group, column_group, i):
        if not plan.mirrored:
            return i
        return 2 * i + lax.rem(m + jnp.where(row_group < column_group, 1, 0), 2)

    parts, step = plan.parts, plan.step

    def slot(o, member, h):
        return tiles[o].at[pl.ds(member * (N + 1) + h * step, step)]

    def cut(group):
        if G == 1:
            return docs
        return docs.at[:, pl.ds(pl.multiple_of(group * L, L), L)]

    first = [o for o in range(1, G) if plan.stage(o) == 1]
    second = [o for o in range(1, G) if plan.stage(o) == 2]
    loads = {}
    for o in first + [0] + second:
        loads[o] = pltpu.make_async_copy(cut(groups[o]), raw[o], raw_sem.at[o])
        loads[o].start()

    barrier = pltpu.get_barrier_semaphore()
    greeted = [
        (o, u) for o in range(D) for u in range(T) if o + u and (plan.mirrored or not o * u)
    ]
    for o, u in greeted:
        pl.semaphore_signal(
            barrier, inc=1, device_id=(doc_peer(o), term_peer(u)), device_id_type=MESH
        )
    pending = []

    def begin(copy):
        copy.start()
        pending.append(copy)
        return copy

    def send_range(o, h):
        return begin(
            remote(
                ranges[o].at[pl.ds(h * step, step)], slot(o, m, h), send_a.at[o, h],
                recv_a.at[o, m, h], groups[o] * M + m, t,
            )
        )

    def hand_on(o, h):
        for i in range(1, M):
            begin(
                remote(
                    slot(o, m, h), slot(o, m, h), send_f.at[o, i, h], recv_a.at[o, m, h],
                    g * M + sibling(i), t,
                )
            )

    def take_over(o):
        for h in range(parts):
            for i in range(1, M):
                other = sibling(i)
                remote(
                    slot(o, other, h), slot(o, other, h), send_f.at[o, i, h], recv_a.at[o, other, h],
                    g * M + other, t,
                ).wait_recv()

    def arrived(o, h):
        remote(
            slot(o, m, h), slot(o, m, h), send_a.at[o, h], recv_a.at[o, m, h], groups[o] * M + m, t
        ).wait_recv()
        hand_on(o, h)

    def slots_first(o):
        loads[o].wait()

        def some_rows(k, carry):
            rows = pl.ds(pl.multiple_of(k * plan.rows, plan.rows), plan.rows)
            held = raw[o][pl.ds(pl.multiple_of(k * plan.rows * N, plan.rows * N), plan.rows * N), :]
            value = jnp.dot(order[...], held, preferred_element_type=jnp.float32)
            value = value.astype(docs.dtype).reshape(N, plan.rows, L)
            if o:
                ranges[o][:, rows, :] = value
            else:
                tiles[0][pl.ds(m * (N + 1), N), rows, :] = value
            return carry

        lax.fori_loop(0, R // plan.rows, some_rows, 0)

    size = plan.rows * N
    origin = jnp.concatenate(
        [lax.broadcasted_iota(jnp.int32, (plan.rows, 1), 0) * N + a for a in range(N)], axis=0
    )
    hit = origin == lax.broadcasted_iota(jnp.int32, (size, size), 1)
    order[...] = jnp.where(hit, 1.0, 0.0).astype(docs.dtype)

    first_sends = []
    if first:
        slots_first(first[0])
    if greeted:
        pl.semaphore_wait(barrier, len(greeted))
    for o in first:
        if o != first[0]:
            slots_first(o)
        for h in range(parts):
            first_sends.append(send_range(o, h))
    slots_first(0)
    for h in range(parts):
        hand_on(0, h)
    for o in second:
        slots_first(o)
        for h in range(parts - 1):
            send_range(o, h)

    for o in range(G):
        tiles[o][m * (N + 1) + N] = jnp.zeros((R, L), docs.dtype)
    same = lax.broadcasted_iota(jnp.int32, (N, N), 0) == lax.broadcasted_iota(jnp.int32, (N, N), 1)
    place = lax.broadcasted_iota(jnp.int32, (N, N), 0)
    for a in range(G):
        line = names[pl.ds(groups[a] * M + m, 1), :]
        upright = jnp.sum(jnp.where(same, line, 0), axis=1, keepdims=True)
        for c in range(D):
            found = jnp.where(upright == names[c : c + 1, :], place, N)
            table_rows[a * D + c : a * D + c + 1, 0:N] = jnp.min(found, axis=0, keepdims=True)
    to_scalars = pltpu.make_async_copy(table_rows, table, table_sem)
    to_scalars.start()

    def add_square(a, total):
        for q in range(G):
            held = ranges[q][a] if q else tiles[0][m * (N + 1) + a]
            value = held.astype(jnp.float32)
            total = total + value * value
        return total

    square = lax.fori_loop(0, N, add_square, jnp.zeros((R, L), jnp.float32))
    column = jnp.sum(square, axis=1, keepdims=True)
    eye = lax.broadcasted_iota(jnp.int32, (R, R), 0) == lax.broadcasted_iota(jnp.int32, (R, R), 1)
    row = jnp.sum(jnp.where(eye, column, 0.0), axis=0, keepdims=True)
    sq_term[t] = jnp.broadcast_to(row, (8, R))
    for o in range(1, T):
        begin(remote(sq_term.at[t], sq_term.at[t], send_st.at[o], recv_st.at[t], d, term_peer(o)))
    for o in range(1, T):
        p = term_peer(o)
        remote(sq_term.at[p], sq_term.at[p], send_st.at[o], recv_st.at[p], d, p).wait_recv()
    total = sq_term[0]
    for q in range(1, T):
        total = total + sq_term[q]
    sq_doc[d] = total
    for o in range(1, D):
        begin(remote(sq_doc.at[d], sq_doc.at[d], send_sd.at[o], recv_sd.at[d], doc_peer(o), t))

    def over_term(source, landing, ssem, rsem):
        for o in range(1, T):
            p = term_peer(o)
            begin(
                remote(
                    source.at[:, pl.ds(p * SR, SR), :], landing.at[o - 1], ssem.at[o], rsem.at[o], d, p
                )
            )

    def pair(a, b):
        wave = plan.wave(a, b)
        if plan.term_first(a, b):
            target, base = early[wave, a], plan.blocks(wave, a).index((b, 0))
        else:
            target, base = part[a, b], 0

        def one(i, carry):
            member = i if a == b else column_member(groups[a], groups[b], i)
            line = a * D + groups[b] * M + member
            left = jnp.concatenate(
                [tiles[a][m * (N + 1) + table[line, e]] for e in range(N)], axis=1
            )
            right = jnp.concatenate([tiles[b][member * (N + 1) + e] for e in range(N)], axis=1)
            target[base + i] = lax.dot_general(
                left, right, (((1,), (1,)), ((), ())), preferred_element_type=jnp.float32
            )
            return carry

        number = plan.count(a ^ b)
        if number == 1:
            one(0, 0)
        else:
            lax.fori_loop(0, number, one, 0)
        if plan.term_first(a, b):
            if plan.blocks(wave, a)[-1][0] == b:
                over_term(
                    early[wave, a], early_z[wave, a], send_ez.at[wave - 1, a], recv_ez.at[wave - 1, a]
                )
        elif a:
            begin(
                remote(
                    part[a, b], got[a, b], send_p.at[a, b], recv_p.at[a, b], groups[a] * M + m, t
                )
            )

    wanted = list(range(1, G)) + [0]

    def pairs(stage):
        todo = [
            (a, b)
            for a in range(G)
            for b in range(G)
            if plan.wave(a, b) == stage
        ]
        for a, b in [p for p in todo if plan.term_first(*p)]:
            pair(a, b)
        rest = [p for p in todo if not plan.term_first(*p)]
        for a, b in sorted(rest, key=lambda ab: (wanted.index(ab[0] ^ ab[1]), -ab[0])):
            pair(a, b)

    to_scalars.wait()
    take_over(0)
    pairs(0)
    for h in range(parts):
        for o in first:
            arrived(o, h)
    for copy in first_sends:
        copy.wait_send()
        pending.remove(copy)
    for o in second:
        send_range(o, parts - 1)
    for o in first:
        take_over(o)
    if first:
        pairs(1)
    for h in range(parts):
        for o in second:
            arrived(o, h)
    for o in second:
        take_over(o)
    if second:
        pairs(2)

    def pass_early(wave):
        for w, a in [key for key in plan.sets() if key[0] == wave]:
            for o in range(1, T):
                remote(
                    early[w, a].at[:, pl.ds(t * SR, SR), :], early_z[w, a].at[o - 1],
                    send_ez.at[w - 1, a, o], recv_ez.at[w - 1, a, o], d, term_peer(o),
                ).wait_recv()
            for i in range(len(plan.blocks(w, a))):
                total = early[w, a][i, pl.ds(pl.multiple_of(t * SR, SR), SR), :]
                for o in range(1, T):
                    total = total + early_z[w, a][o - 1, i]
                early_sum[w, a][i] = total
            begin(
                remote(
                    early_sum[w, a], early_xy[w, a], send_ex.at[w - 1, a], recv_ex.at[w - 1, a],
                    groups[a] * M + m, t,
                )
            )

    pass_early(1)
    for b in wanted:
        direct = [a for a in range(1, G) if not plan.term_first(a, a ^ b)]
        for a in direct:
            remote(
                part[a, a ^ b], got[a, a ^ b], send_p.at[a, a ^ b], recv_p.at[a, a ^ b],
                groups[a] * M + m, t,
            ).wait_recv()
        for i in range(plan.count(b)):
            total = part[0, b][i]
            for a in direct:
                total = total + got[a, a ^ b][i]
            whole[b][i] = total
        over_term(whole[b], got_z[b], send_z.at[b], recv_z.at[b])
    pass_early(2)

    def mirror_member(b, i):
        return 2 * i + lax.rem(m + jnp.where(groups[b] < g, 1, 0), 2)

    lane_set = lax.div(lax.broadcasted_iota(jnp.int32, (max(SR // T, 1), R), 1), SR)
    for w, a in plan.sets():
        remote(
            early_sum[w, a], early_xy[w, a], send_ex.at[w - 1, a], recv_ex.at[w - 1, a],
            groups[a] * M + m, t,
        ).wait_recv()
    sums = {}
    for b in wanted:
        for o in range(1, T):
            remote(
                whole[b].at[:, pl.ds(t * SR, SR), :], got_z[b].at[o - 1], send_z.at[b, o],
                recv_z.at[b, o], d, term_peer(o),
            ).wait_recv()
        for i in range(plan.count(b)):
            total = whole[b][i, pl.ds(pl.multiple_of(t * SR, SR), SR), :]
            for o in range(1, T):
                total = total + got_z[b][o - 1, i]
            for a in range(1, G):
                if plan.term_first(a, a ^ b):
                    wave = plan.wave(a, a ^ b)
                    total = total + early_xy[wave, a][plan.blocks(wave, a).index((a ^ b, i))]
            sums[b, i] = total
            if plan.mirrored and b:
                upright = jnp.concatenate([total] * T, axis=0).T
                size = SR // T
                for u in range(T):
                    packed = jnp.zeros((size, R), jnp.float32)
                    for k in range(T):
                        lines = upright[u * SR + k * size : u * SR + (k + 1) * size]
                        packed = jnp.where(lane_set == k, lines, packed)
                    turned[b][i, u] = packed
                for w in range(T):
                    u = term_peer(w)
                    begin(
                        remote(
                            turned[b].at[i, u], mirror[b].at[lax.div(m, 2), t], send_m.at[b, i, w],
                            recv_m.at[b, lax.div(m, 2), t],
                            groups[b] * M + column_member(g, groups[b], i), u,
                        )
                    )

    for o in range(1, D):
        p = doc_peer(o)
        remote(sq_doc.at[p], sq_doc.at[p], send_sd.at[o], recv_sd.at[p], p, t).wait_recv()
    pick = lax.broadcasted_iota(jnp.int32, (SR, R), 1) == (
        lax.broadcasted_iota(jnp.int32, (SR, R), 0) + t * SR
    )
    own_column = jnp.sum(jnp.where(pick, sq_doc[d][0:1], 0.0), axis=1, keepdims=True)
    row_norm = jnp.sqrt(own_column + epsilon)

    def finish(total, c):
        norms = row_norm * jnp.sqrt(sq_doc[c][0:1] + epsilon)
        out[:, pl.ds(pl.multiple_of(c * R, R), R)] = total / norms

    for b, i in sums:
        finish(sums[b, i], groups[b] * M + (column_member(g, groups[b], i) if b else i))
    if plan.mirrored:
        for b in range(1, G):
            for i in range(H):
                c = groups[b] * M + mirror_member(b, i)
                for u in range(T):
                    remote(
                        turned[b].at[i, u], mirror[b].at[i, u], send_m.at[b, i, u],
                        recv_m.at[b, i, u], c, t,
                    ).wait_recv()
                lines = []
                for k in range(T):
                    line = jnp.zeros((SR // T, R), jnp.float32)
                    for u in range(T):
                        piece = mirror[b][i, u]
                        if u != k:
                            piece = pltpu.roll(piece, (u - k) % T * SR, 1)
                        line = jnp.where(lane_set == u, piece, line)
                    lines.append(line)
                finish(jnp.concatenate(lines, axis=0), c)

    for copy in pending:
        copy.wait_send()


def shards(doc_tiles, tile_list):
    D = lax.axis_size("doc")
    T = lax.axis_size("term")
    R, N, W = doc_tiles.shape
    plan = Plan(D, T, R, N, W)
    G, M, H, L, SR = plan.G, plan.M, plan.H, plan.L, plan.SR
    many = lambda *shape: pltpu.SemaphoreType.DMA(shape)
    buffer = lambda *shape: pltpu.VMEM(tuple(max(n, 1) for n in shape), jnp.float32)
    scratch = [pltpu.VMEM((M * (N + 1), R, L), doc_tiles.dtype) for _ in range(G)]
    numbers = [len(plan.blocks(*key)) for key in plan.sets()]
    scratch += [buffer(plan.count(a ^ b), R, R) for a, b in plan.direct()]
    scratch += [buffer(plan.count(a ^ b), R, R) for a, b in plan.direct() if a]
    scratch += [buffer(n, R, R) for n in numbers]
    scratch += [buffer(T - 1, n, SR, R) for n in numbers]
    scratch += [buffer(n, SR, R) for n in numbers]
    scratch += [buffer(n, SR, R) for n in numbers]
    scratch += [buffer(plan.count(b), R, R) for b in range(G)]
    scratch += [buffer(T - 1, plan.count(b), SR, R) for b in range(G)]
    if plan.mirrored:
        scratch += [buffer(H, T, SR // T, R) for _ in range(1, G)]
        scratch += [buffer(H, T, SR // T, R) for _ in range(1, G)]
    scratch += [pltpu.VMEM((R * N, L), doc_tiles.dtype) for _ in range(G)]
    scratch += [pltpu.VMEM((N, R, L), doc_tiles.dtype) for _ in range(1, G)]
    scratch += [pltpu.VMEM((plan.rows * N, plan.rows * N), doc_tiles.dtype)]
    scratch += [buffer(T, 8, R), buffer(D, 8, R)]
    scratch += [pltpu.VMEM((G * D, LANES), jnp.int32), pltpu.SMEM((G * D, LANES), jnp.int32)]
    scratch += [
        many(G), pltpu.SemaphoreType.DMA,
        many(G, plan.parts), many(G, M, plan.parts), many(G, M, plan.parts),
        many(T), many(T), many(D), many(D),
        many(G, G), many(G, G), many(G, M, T), many(G, M, T),
        many(G, T), many(G, T), many(2, G, T), many(2, G, T), many(2, G), many(2, G),
    ]
    return pl.pallas_call(
        functools.partial(body, plan),
        out_shape=jax.ShapeDtypeStruct((SR, D * R), jnp.float32),
        in_specs=[
            pl.BlockSpec(memory_space=pltpu.VMEM),
            pl.BlockSpec(memory_space=pl.ANY),
        ],
        out_specs=pl.BlockSpec(memory_space=pltpu.VMEM),
        scratch_shapes=scratch,
        compiler_params=pltpu.CompilerParams(
            collective_id=0, has_side_effects=True, vmem_limit_bytes=56 * 1024 * 1024
        ),
        cost_estimate=pl.CostEstimate(
            flops=2 * G * R * D * R * N * L,
            bytes_accessed=R * N * W * 2 + SR * D * R * 4,
            transcendentals=0,
        ),
    )(tile_list, doc_tiles.reshape(R * N, W))


def solution(mesh):
    placed = (P("doc", None, "term"), P())
    return jax.shard_map(
        shards, mesh=mesh, in_specs=placed, out_specs=P(("doc", "term"), None), check_vma=False
    )
```
